32 devices in a mesh: gz: 8 (over z, y), ky: 4 (over x, core).
Axes of the slice: x: 2, y: 2, z: 4, core: 2. Of those that a mesh axis runs over, the one named last changes fastest.
Arguments:
- fields: bfloat16 [256, 3, 2, 32768], P('gz', None, None, 'ky'), may hold values from -6 to 6
- wall_operator: bfloat16 [256, 256], replicated, may hold values from -0.375 to 0.375
- remap_offset: int32 [4, 4], replicated, may hold values from 0 to 31, as said below
- remap_count: int32 [4, 4], replicated, may hold values from 1 to 8, as said below
Outputs:
- spectra: float32 [256, 3, 2, 32768], P('gz', None, None, 'ky')
The draws below stay inside these ranges and needn't reach their ends.
Inputs may be any that keep to these rules, and one draw needn't show every extreme that they name: remap_count[g, h] rows go from group g to group h; in every draw one group h receives exactly 8 rows from every group. The run from group g to group h is rows remap_offset[g, h] to remap_offset[g, h] + remap_count[g, h] - 1 of group g's 32 rows; the runs of one group do not intersect.
All inputs are finite; a program needn't handle non-finite values.
Results may differ from the reference program's by a relative error of at most 0.0048.
Values may be sent and summed in bfloat16 or wider, within the bound.
No kernel may reach another device: no remote copies, remote signals or barrier semaphores. Data moves between devices by JAX's collectives and lax.ppermute only.
A program may use at most 128 MiB of HBM per device.

```python
import math
import jax
import jax.numpy as jnp
from jax import lax

NX = 256
ROWS_DEV = 32
NZ = 256
GROUPS = 4
SLOT = 8
ROWS = 128


def remap_tables(key):
    count_key, column_key, order_key, shift_key, group_key = jax.random.split(key, 5)
    counts = jax.random.randint(count_key, (GROUPS, GROUPS), 1, SLOT + 1)
    full_column = jax.random.randint(column_key, (), 0, GROUPS)
    column_index = jnp.arange(GROUPS, dtype=jnp.int32)
    group_index = jnp.arange(GROUPS, dtype=jnp.int32)
    counts = jnp.where(column_index[None, :] == full_column, SLOT, counts).astype(jnp.int32)
    last_group = jax.random.randint(group_key, (), 0, GROUPS)
    last_column = (full_column + 1) % GROUPS
    single = (group_index[:, None] == last_group) & (column_index[None, :] == last_column)
    counts = jnp.where(single, 1, counts).astype(jnp.int32)
    order_keys = jax.random.split(order_key, GROUPS)
    ranking = jax.vmap(jax.random.permutation, in_axes=(0, None))(order_keys, GROUPS).astype(jnp.int32)
    target_rank = jnp.sum(jnp.where(column_index == last_column, ranking[last_group], 0))
    moved_row = jnp.where(ranking[last_group] == GROUPS - 1, target_rank, ranking[last_group])
    moved_row = jnp.where(column_index == last_column, GROUPS - 1, moved_row)
    ranking = jnp.where(group_index[:, None] == last_group, moved_row[None, :], ranking).astype(jnp.int32)
    preceding = (ranking[:, None, :] < ranking[:, :, None]).astype(jnp.int32)
    start_rows = jnp.sum(preceding * counts[:, None, :], axis=2).astype(jnp.int32)
    spare_rows = (ROWS_DEV - jnp.sum(counts, axis=1)).astype(jnp.int32)
    shift_rows = jax.random.randint(shift_key, (GROUPS,), 0, spare_rows + 1).astype(jnp.int32)
    shift_rows = jnp.where(group_index == last_group, spare_rows, shift_rows)
    shift_rows = jnp.where(group_index == (last_group + 1) % GROUPS, 0, shift_rows).astype(jnp.int32)
    offsets = (shift_rows[:, None] + start_rows).astype(jnp.int32)
    return (offsets, counts)


def draw_remap_offset(key, part):
    offsets, counts = remap_tables(key)
    return offsets


def draw_remap_count(key, part):
    offsets, counts = remap_tables(key)
    return counts


def levels(stream_key, dims, cuts, smallest, largest):
    level, own = 1.0, jax.random.fold_in(stream_key, 6)
    for dim, parts in cuts:
        heights = jnp.exp(jax.random.uniform(jax.random.fold_in(own, dim), (parts,), jnp.float32, smallest / len(cuts), largest / len(cuts)))
        level = level * jnp.repeat(heights, dims[dim] // parts).reshape([-1 if axis == dim else 1 for axis in range(len(dims))])
    return level


def gaussian(own_key, dims, width, reach, cuts=(), kind=jnp.bfloat16):
    entries = width * jax.random.normal(own_key, dims, jnp.float32)
    if cuts:
        entries = entries * levels(own_key, dims, cuts, -0.22, 0.18)
    return jnp.clip(entries, -reach, reach).astype(kind)


def setup_inputs(seed: int = 0) -> dict:
    key_of = jax.random.split(jax.random.key(seed), 5)
    fields = gaussian(key_of[0], (NZ, 3, 2, ROWS * NX), 1.0, 6.0, ((0, 8), (3, 4)))
    wall_operator = gaussian(key_of[1], (NX, NX), NX ** -0.5, 0.375)
    remap_offset = draw_remap_offset(jax.random.fold_in(key_of[4], 71), 0)
    remap_count = draw_remap_count(jax.random.fold_in(key_of[4], 71), 0)
    return {"fields": fields, "wall_operator": wall_operator, "remap_offset": remap_offset, "remap_count": remap_count}


NU_COEF = 0.05
STEP_DT = 0.3

def mode_tables(half_z):
    row_index = jnp.arange(half_z, dtype=jnp.int32)[:, None]
    column_index = jnp.arange(half_z, dtype=jnp.int32)[None, :]
    norm_factor = math.sqrt(2.0 / half_z)
    angle_step = math.pi / (2 * half_z)
    cos_index = row_index * (2 * column_index + 1) % (4 * half_z)
    sin_index = (row_index + 1) * (2 * (half_z - 1 - column_index) + 1) % (4 * half_z)
    cos_table = (norm_factor * jnp.cos(cos_index.astype(jnp.float32) * angle_step)).astype(jnp.bfloat16)
    sin_table = (norm_factor * jnp.sin(sin_index.astype(jnp.float32) * angle_step)).astype(jnp.bfloat16)
    return (cos_table, sin_table)

def couple(mode_values, half_z):
    total_z = mode_values.shape[0]
    mode_index = jnp.arange(total_z, dtype=jnp.int32)
    wave_index = jnp.where(mode_index < half_z, mode_index, mode_index - half_z + 1)
    wave_number = wave_index.astype(jnp.float32) * (math.pi / half_z)
    wave_number = wave_number.reshape((total_z,) + (1,) * (mode_values.ndim - 2))
    damping = jnp.exp(-NU_COEF * wave_number * wave_number)
    velocity = mode_values[:, 0]
    buoyant = mode_values[:, 1]
    magnetic = mode_values[:, 2]
    new_velocity = damping * (velocity + STEP_DT * buoyant + STEP_DT * wave_number * magnetic)
    new_buoyant = damping * (buoyant - STEP_DT * velocity)
    new_magnetic = damping * (magnetic - STEP_DT * wave_number * velocity)
    return jnp.stack([new_velocity, new_buoyant, new_magnetic], axis=1)

def remap_index(offsets, counts, row_stride, rows_out):
    counts = counts.astype(jnp.int32)
    start_rows = (jnp.cumsum(counts) - counts).astype(jnp.int32)
    position = jnp.arange(rows_out, dtype=jnp.int32)
    inside = (position[None, :] >= start_rows[:, None]) & (position[None, :] < (start_rows + counts)[:, None])
    group_index = jnp.arange(counts.shape[0], dtype=jnp.int32)
    source = group_index[:, None] * row_stride + offsets[:, None] + position[None, :] - start_rows[:, None]
    chosen = lax.optimization_barrier(jnp.sum(jnp.where(inside, source, 0), axis=0)).astype(jnp.int32)
    is_valid = jnp.any(inside, axis=0)
    return (chosen, is_valid)

def reference(fields, wall_operator, remap_offset, remap_count):
    total_z = fields.shape[0]
    half_z = total_z // 2
    groups = remap_count.shape[0]
    rows_dev = fields.shape[3] // (groups * NX)
    planes = fields.reshape(total_z, 3, 2, groups * rows_dev, NX)
    index_list = []
    valid_list = []
    for receiver in range(groups):
        chosen, is_valid = remap_index(remap_offset[:, receiver].astype(jnp.int32), remap_count[:, receiver], rows_dev, rows_dev)
        index_list.append(chosen)
        valid_list.append(is_valid)
    chosen_all = jnp.concatenate(index_list).astype(jnp.int32)
    valid_all = jnp.concatenate(valid_list)
    remapped = jnp.take(planes, chosen_all, axis=3)
    remapped = jnp.where(valid_all[None, None, None, :, None], remapped, jnp.zeros((), jnp.bfloat16))
    walled = jnp.einsum('zfcrx,xy->zfcry', remapped.astype(jnp.float32), wall_operator.astype(jnp.float32)).astype(jnp.bfloat16)
    flipped = walled[::-1]
    even_part = 0.5 * (walled[:half_z].astype(jnp.float32) + flipped[:half_z].astype(jnp.float32))
    odd_part = 0.5 * (flipped[half_z:].astype(jnp.float32) - walled[half_z:].astype(jnp.float32))
    parity = jnp.concatenate([even_part, odd_part]).astype(jnp.bfloat16)
    cos_table, sin_table = mode_tables(half_z)
    flat_parity = parity.reshape(total_z, -1).astype(jnp.float32)
    cosine = jnp.dot(cos_table.astype(jnp.float32), flat_parity[:half_z], precision=lax.Precision.HIGHEST)
    sine_part = jnp.dot(sin_table.astype(jnp.float32), flat_parity[half_z:], precision=lax.Precision.HIGHEST)
    mode_values = jnp.concatenate([cosine, sine_part]).reshape(total_z, 3, 2, -1)
    spectra = couple(mode_values, half_z)
    return spectra.reshape(total_z, 3, 2, groups * rows_dev * NX)
```

```python
import math

import jax
import jax.numpy as jnp
import ml_dtypes
import numpy as np
from jax import lax
from jax.experimental import pallas as pl
from jax.experimental.pallas import tpu as pltpu
from jax.sharding import PartitionSpec as P

NU_COEF = 0.05
STEP_DT = 0.3
SLOT = 8
ORDER = (2, 3, 1, 0)
BF16 = jnp.bfloat16
F32 = jnp.float32


def mode_matrix(half_z):
    row = np.arange(half_z)[:, None]
    column = np.arange(half_z)[None, :]
    norm = math.sqrt(2.0 / half_z)
    step = math.pi / (2 * half_z)
    cosine = norm * np.cos(((row * (2 * column + 1)) % (4 * half_z)) * step)
    sine = norm * np.sin((((row + 1) * (2 * (half_z - 1 - column) + 1)) % (4 * half_z)) * step)
    cosine = cosine.astype(np.float32).astype(ml_dtypes.bfloat16).astype(np.float32)
    sine = sine.astype(np.float32).astype(ml_dtypes.bfloat16).astype(np.float32)
    top = np.concatenate([0.5 * cosine, 0.5 * cosine[:, ::-1]], axis=1)
    bottom = np.concatenate([0.5 * sine[:, ::-1], -0.5 * sine], axis=1)
    whole = np.concatenate([top, bottom], axis=0)
    return np.kron(whole, np.eye(2, dtype=np.float32)).astype(ml_dtypes.bfloat16)


def mode_factors(half_z):
    index = np.arange(2 * half_z)
    wave = np.where(index < half_z, index, index - half_z + 1) * (math.pi / half_z)
    pair = np.stack([np.exp(-NU_COEF * wave * wave), STEP_DT * wave]).astype(np.float32)
    return np.broadcast_to(np.repeat(pair, 2, axis=1)[:, :, None], (2, 4 * half_z, 128)).copy()


def wall_rows(fields, wall_operator, source):
    rows, width = source.shape[0], wall_operator.shape[0]
    planes = fields.shape[0]

    def body(source_ref, fields_ref, wall_ref, out_ref):
        for field in range(3):
            block = fields_ref[:, field].reshape(2 * planes, width)
            walled = jnp.dot(block, wall_ref[...], preferred_element_type=F32).astype(BF16)
            for half in range(2):
                out_ref[half, field] = walled[:, half * 128 : half * 128 + 128]

    return pl.pallas_call(
        body,
        grid_spec=pltpu.PrefetchScalarGridSpec(
            num_scalar_prefetch=1,
            grid=(rows,),
            in_specs=[
                pl.BlockSpec((planes, 3, 2, width), lambda i, source: (0, 0, 0, source[i])),
                pl.BlockSpec((width, width), lambda i, source: (0, 0)),
            ],
            out_specs=pl.BlockSpec((2, 3, 2 * planes, 128), lambda i, source: (i, 0, 0, 0)),
        ),
        out_shape=jax.ShapeDtypeStruct((2 * rows, 3, 2 * planes, 128), BF16),
        cost_estimate=pl.CostEstimate(
            flops=rows * 12 * planes * width * width, bytes_accessed=rows * 24 * planes * width, transcendentals=0
        ),
    )(source, fields, wall_operator)


def transform(pencil, matrix, factors):
    devices, units, _, depth, lanes = pencil.shape
    size = devices * depth

    def body(pencil_ref, matrix_ref, factors_ref, out_ref):
        block = jnp.concatenate([pencil_ref[:, 0, f].reshape(size, lanes) for f in range(3)], axis=1)
        modes = jnp.dot(matrix_ref[...], block, preferred_element_type=F32)
        velocity, buoyant, magnetic = (modes[:, f * lanes : f * lanes + lanes] for f in range(3))
        damping, wave = factors_ref[0], factors_ref[1]
        coupled = (
            damping * (velocity + STEP_DT * buoyant + wave * magnetic),
            damping * (buoyant - STEP_DT * velocity),
            damping * (magnetic - wave * velocity),
        )
        for f in range(3):
            out_ref[:, 0, f] = coupled[f].astype(BF16).reshape(devices, depth, lanes)

    block = pl.BlockSpec((devices, 1, 3, depth, lanes), lambda u: (0, u, 0, 0, 0))
    return pl.pallas_call(
        body,
        grid=(units,),
        in_specs=[
            block,
            pl.BlockSpec((size, size), lambda u: (0, 0)),
            pl.BlockSpec((2, size, lanes), lambda u: (0, 0, 0)),
        ],
        out_specs=block,
        out_shape=jax.ShapeDtypeStruct(pencil.shape, BF16),
        compiler_params=pltpu.CompilerParams(vmem_limit_bytes=48 * 2**20),
        cost_estimate=pl.CostEstimate(
            flops=units * 6 * size * size * lanes, bytes_accessed=units * 12 * size * lanes, transcendentals=0
        ),
    )(pencil, matrix, factors)


def place_rows(parts, chosen, places, rows_dev, width):
    depth, lanes = parts[0].shape[2], parts[0].shape[3]
    planes = depth // 2

    def body(chosen_ref, places_ref, *refs):
        out_ref = refs[-1]
        choice = chosen_ref[pl.program_id(0)]
        for c in range(len(parts)):

            @pl.when(choice == c)
            def _(part_ref=refs[c]):
                for half in range(2):
                    for field in range(3):
                        out_ref[:, field, :, half * lanes : half * lanes + lanes] = (
                            part_ref[half, field].astype(F32).reshape(planes, 2, lanes)
                        )

        @pl.when(choice < 0)
        def _():
            out_ref[...] = jnp.zeros_like(out_ref)

    def part_spec(c):
        return pl.BlockSpec((2, 3, depth, lanes), lambda r, chosen, places: (places[c, r], 0, 0, 0))

    return pl.pallas_call(
        body,
        grid_spec=pltpu.PrefetchScalarGridSpec(
            num_scalar_prefetch=2,
            grid=(rows_dev,),
            in_specs=[part_spec(c) for c in range(len(parts))],
            out_specs=pl.BlockSpec((planes, 3, 2, width), lambda r, chosen, places: (0, 0, 0, r)),
        ),
        out_shape=jax.ShapeDtypeStruct((planes, 3, 2, rows_dev * width), F32),
        cost_estimate=pl.CostEstimate(
            flops=0, bytes_accessed=rows_dev * 36 * planes * width, transcendentals=0
        ),
    )(chosen, places, *parts)


def run(rows, fields, wall_operator, remap_offset, remap_count, matrix, factors):
    gz = lax.axis_size("gz")
    group = lax.axis_index("ky")
    width = wall_operator.shape[0]
    rows_dev = fields.shape[3] // width
    chunks = (2 * SLOT, rows - 2 * SLOT)
    order = jnp.array(ORDER, jnp.int32)

    receivers = group ^ order
    counts = remap_count[group, receivers]
    offsets = remap_offset[group, receivers]
    ends = jnp.cumsum(counts)
    starts = ends - counts
    position = jnp.arange(rows, dtype=jnp.int32)
    inside = (position[None] >= starts[:, None]) & (position[None] < ends[:, None])
    source = jnp.sum(jnp.where(inside, offsets[:, None] + position[None] - starts[:, None], 0), axis=0)

    returned, first = [], 0
    for chunk in chunks:
        walled = wall_rows(fields, wall_operator, source[first : first + chunk])
        first += chunk
        pencil = lax.all_to_all(walled, "gz", split_axis=0, concat_axis=0, tiled=True)
        pencil = pencil.reshape((gz, -1) + pencil.shape[1:])
        modes = transform(pencil, matrix, factors)
        modes = modes.reshape((-1,) + modes.shape[2:])
        returned.append(lax.all_to_all(modes, "gz", split_axis=0, concat_axis=0, tiled=True))

    done = (returned[0], returned[0], jnp.concatenate(returned))
    parts = []
    for j, flip in enumerate(ORDER[:-1]):
        base = jnp.minimum(starts[j], done[j].shape[0] // 2 - SLOT)
        window = lax.dynamic_slice_in_dim(done[j], 2 * base, 2 * SLOT, axis=0)
        pairs = [(g, g ^ flip) for g in range(lax.axis_size("ky"))]
        parts.append(lax.ppermute(window, "ky", pairs))
    parts += returned

    senders = group ^ order
    got = remap_count[:, group]
    got_start = (jnp.cumsum(got) - got)[senders]
    got = got[senders]
    sent_counts = remap_count[senders[:, None], senders[:, None] ^ order[None]]
    sent_start = jnp.sum(jnp.where(jnp.tri(4, 4, -1, dtype=bool), sent_counts, 0), axis=1)
    limits = jnp.array([d.shape[0] // 2 - SLOT for d in done] + [rows], jnp.int32)
    shift = jnp.where(order == 0, sent_start, sent_start - jnp.minimum(sent_start, limits))
    row = jnp.arange(rows_dev, dtype=jnp.int32)
    from_sender = row[None] - got_start[:, None]
    held = (from_sender >= 0) & (from_sender < got[:, None])
    place = jnp.clip(from_sender, 0, got[:, None] - 1) + shift[:, None]
    own = len(ORDER) - 1
    which = jnp.arange(own + 1, dtype=jnp.int32)[:, None]
    chosen = jnp.sum(jnp.where(held, which + 1, 0), axis=0) - 1
    chosen = jnp.where((chosen == own) & (place[own] >= chunks[0]), own + 1, chosen)
    places = jnp.concatenate([
        place[:own],
        jnp.clip(place[own:], 0, chunks[0] - 1),
        jnp.clip(place[own:] - chunks[0], 0, chunks[1] - 1),
    ])
    return place_rows(parts, chosen, places, rows_dev, width)


def per_device(fields, wall_operator, remap_offset, remap_count):
    half_z = fields.shape[0] * lax.axis_size("gz") // 2
    matrix = jnp.asarray(mode_matrix(half_z))
    factors = jnp.asarray(mode_factors(half_z))
    rows_dev = fields.shape[3] // wall_operator.shape[0]
    return run(rows_dev, fields, wall_operator, remap_offset, remap_count, matrix, factors)


def solution(mesh):
    placed = (P("gz", None, None, "ky"), P(), P(), P())
    return jax.shard_map(
        per_device, mesh=mesh, in_specs=placed, out_specs=P("gz", None, None, "ky"), check_vma=False
    )
```

```python
import math

import jax
import jax.numpy as jnp
import ml_dtypes
import numpy as np
from jax import lax
from jax.experimental import pallas as pl
from jax.experimental.pallas import tpu as pltpu
from jax.sharding import PartitionSpec as P

NU_COEF = 0.05
STEP_DT = 0.3
SLOT = 8
LANES = 128
ORDER = (2, 3, 1, 0)
BF16 = jnp.bfloat16
F32 = jnp.float32
PARAMS = pltpu.CompilerParams(vmem_limit_bytes=56 * 2**20)


def mode_matrix(half_z):
    row = np.arange(half_z)[:, None]
    column = np.arange(half_z)[None, :]
    norm = math.sqrt(2.0 / half_z)
    step = math.pi / (2 * half_z)
    cosine = norm * np.cos(((row * (2 * column + 1)) % (4 * half_z)) * step)
    sine = norm * np.sin((((row + 1) * (2 * (half_z - 1 - column) + 1)) % (4 * half_z)) * step)
    cosine = cosine.astype(np.float32).astype(ml_dtypes.bfloat16).astype(np.float32)
    sine = sine.astype(np.float32).astype(ml_dtypes.bfloat16).astype(np.float32)
    top = np.concatenate([0.5 * cosine, 0.5 * cosine[:, ::-1]], axis=1)
    bottom = np.concatenate([0.5 * sine[:, ::-1], -0.5 * sine], axis=1)
    whole = np.concatenate([top, bottom], axis=0)
    return np.kron(whole, np.eye(2, dtype=np.float32)).astype(ml_dtypes.bfloat16)


def mode_factors(half_z):
    index = np.arange(2 * half_z)
    wave = np.where(index < half_z, index, index - half_z + 1) * (math.pi / half_z)
    pair = np.stack([np.exp(-NU_COEF * wave * wave), STEP_DT * wave]).astype(np.float32)
    return np.broadcast_to(np.repeat(pair, 2, axis=1)[:, :, None], (2, 4 * half_z, LANES)).copy()


def run_starts(count_ref, group):
    starts = [0]
    for flip in ORDER:
        starts.append(starts[-1] + count_ref[group, group ^ flip])
    return starts


def hbm_spec():
    return pl.BlockSpec(memory_space=pl.ANY)


def whole_spec(shape):
    return pl.BlockSpec(shape, lambda *_: (0,) * len(shape))


def wall_rows(first, rows, devices, tables, fields, wall_operator):
    width = wall_operator.shape[0]
    planes = fields.shape[0]
    depth = 2 * planes
    units = 2 * rows // devices
    pairs = max(1, units // 2) if units != 3 else 3

    def body(me_ref, offset_ref, count_ref, fields_ref, wall_ref, *refs):
        outs, held = refs[:devices], refs[devices]
        me, group = me_ref[0], me_ref[1]
        starts = run_starts(count_ref, group)

        def source(i):
            row = 0
            for j, flip in enumerate(ORDER):
                here = offset_ref[group, group ^ flip] + i - starts[j]
                row = jnp.where((i >= starts[j]) & (i < starts[j + 1]), here, row)
            return row

        for s in range(devices):
            if units % 2 == 0:
                wanted = [(first + (me ^ s) * pairs + v, None) for v in range(pairs)]
            else:
                wanted = [
                    (first + lax.shift_right_logical(unit, 1), unit & 1)
                    for unit in ((me ^ s) * units + u for u in range(units))
                ]
            for v, (i, _) in enumerate(wanted):
                column = pl.multiple_of(source(i) * width, width)
                for field in range(3):
                    at = (v * 3 + field) * depth
                    held[at : at + depth] = fields_ref[:, field, :, pl.ds(column, width)].reshape(depth, width)
            if units % 2 == 0:
                walled = jnp.dot(held[...], wall_ref[...], preferred_element_type=F32).astype(BF16)
                for v in range(pairs):
                    for field in range(3):
                        at = (v * 3 + field) * depth
                        for half in range(2):
                            outs[s][2 * v + half, field] = walled[at : at + depth, half * LANES : half * LANES + LANES]
            else:
                for u, (_, half) in enumerate(wanted):
                    wall = wall_ref[:, pl.ds(pl.multiple_of(half * LANES, LANES), LANES)]
                    block = held[u * 3 * depth : (u + 1) * 3 * depth]
                    walled = jnp.dot(block, wall, preferred_element_type=F32).astype(BF16)
                    for field in range(3):
                        outs[s][u, field] = walled[field * depth : field * depth + depth]

    shape = (units, 3, depth, LANES)
    return pl.pallas_call(
        body,
        grid_spec=pltpu.PrefetchScalarGridSpec(
            num_scalar_prefetch=3,
            grid=(1,),
            in_specs=[whole_spec(fields.shape), whole_spec(wall_operator.shape)],
            out_specs=[whole_spec(shape)] * devices,
            scratch_shapes=[pltpu.VMEM((pairs * 3 * depth, width), BF16)],
        ),
        out_shape=[jax.ShapeDtypeStruct(shape, BF16)] * devices,
        compiler_params=PARAMS,
        cost_estimate=pl.CostEstimate(
            flops=rows * 12 * planes * width * width, bytes_accessed=12 * planes * width * (rows + 32), transcendentals=0
        ),
    )(*tables, fields, wall_operator)


def transform(me, pencil, matrix, factors):
    devices = len(pencil)
    units, _, depth, lanes = pencil[0].shape
    size = devices * depth
    strip = 3 * lanes

    def body(me_ref, *refs):
        ins, matrix_ref, factors_ref = refs[:devices], refs[devices], refs[devices + 1]
        outs, (block, turned, scale) = refs[devices + 2 : 2 * devices + 2], refs[2 * devices + 2 :]
        for s in range(devices):
            at = pl.ds(pl.multiple_of((me_ref[0] ^ s) * depth, depth), depth)
            turned[s * depth : (s + 1) * depth] = matrix_ref[at]
            for k in range(2):
                scale[k, s * depth : (s + 1) * depth] = factors_ref[k, at]
            for u in range(units):
                for f in range(3):
                    block[at, u * strip + f * lanes : u * strip + f * lanes + lanes] = ins[s][u, f]
        for u in range(units):
            modes = jnp.dot(turned[...], block[:, u * strip : (u + 1) * strip], preferred_element_type=F32)
            velocity, buoyant, magnetic = (modes[:, f * lanes : f * lanes + lanes] for f in range(3))
            damping, wave = scale[0], scale[1]
            coupled = (
                damping * (velocity + STEP_DT * buoyant + wave * magnetic),
                damping * (buoyant - STEP_DT * velocity),
                damping * (magnetic - wave * velocity),
            )
            for f in range(3):
                rounded = coupled[f].astype(BF16)
                for s in range(devices):
                    outs[s][u, f] = rounded[s * depth : (s + 1) * depth]

    spec = whole_spec(pencil[0].shape)
    return pl.pallas_call(
        body,
        grid_spec=pltpu.PrefetchScalarGridSpec(
            num_scalar_prefetch=1,
            grid=(1,),
            in_specs=[spec] * devices + [whole_spec(matrix.shape), whole_spec(factors.shape)],
            out_specs=[spec] * devices,
            scratch_shapes=[
                pltpu.VMEM((size, units * strip), BF16),
                pltpu.VMEM((size, size), BF16),
                pltpu.VMEM((2, size, lanes), F32),
            ],
        ),
        out_shape=[jax.ShapeDtypeStruct(pencil[0].shape, BF16)] * devices,
        compiler_params=PARAMS,
        cost_estimate=pl.CostEstimate(
            flops=units * 6 * size * size * lanes, bytes_accessed=units * 12 * size * lanes, transcendentals=0
        ),
    )(me, *pencil, matrix, factors)


def unit_of(me, s, u, units, first):
    return 2 * first + (me ^ s) * units + u


def windows(which, me, count, chunks):
    buffers = [b for _, chunk in chunks for b in chunk]
    places = [(first, s) for first, chunk in chunks for s in range(len(chunk))]
    shape = (2 * SLOT,) + buffers[0].shape[1:]

    def body(me_ref, count_ref, *refs):
        ins, outs, sem = refs[: len(buffers)], refs[len(buffers) : -1], refs[-1]
        starts = run_starts(count_ref, me_ref[1])

        def each(act):
            for b, (first, s) in enumerate(places):
                units = ins[b].shape[0]
                for u in range(units):
                    unit = unit_of(me_ref[0], s, u, units, first)
                    for o, j in enumerate(which):
                        slot = unit - 2 * starts[j]

                        @pl.when((slot >= 0) & (unit < 2 * starts[j + 1]))
                        def _(b=b, u=u, o=o, slot=slot):
                            act(pltpu.make_async_copy(ins[b].at[u], outs[o].at[slot], sem.at[o, slot]))

        each(lambda copy: copy.start())
        each(lambda copy: copy.wait())

    return pl.pallas_call(
        body,
        grid_spec=pltpu.PrefetchScalarGridSpec(
            num_scalar_prefetch=2,
            grid=(1,),
            in_specs=[hbm_spec()] * len(buffers),
            out_specs=[hbm_spec()] * len(which),
            scratch_shapes=[pltpu.SemaphoreType.DMA((len(which), 2 * SLOT))],
        ),
        out_shape=[jax.ShapeDtypeStruct(shape, BF16)] * len(which),
        cost_estimate=pl.CostEstimate(flops=0, bytes_accessed=2**21 * len(which), transcendentals=0),
    )(me, count, *buffers)


def place_rows(me, count, received, chunks, rows_dev, width):
    devices = len(chunks[0][1])
    buffers = list(received) + [b for _, chunk in chunks for b in chunk]
    sizes = [b.shape[0] for b in buffers]
    firsts = [sum(sizes[:b]) for b in range(len(sizes) + 1)]
    blank = firsts[-1]
    depth, lanes = buffers[0].shape[2:]
    planes, step = depth // 2, 8

    def body(me_ref, count_ref, *refs):
        ins, out_ref, held, sem = refs[: len(buffers)], refs[-3], refs[-2], refs[-1]
        me, group = me_ref[0], me_ref[1]

        @pl.when(pl.program_id(0) == 0)
        def _():
            copies = [
                pltpu.make_async_copy(ins[b], held.at[pl.ds(firsts[b], sizes[b])], sem.at[b])
                for b in range(len(buffers))
            ]
            for copy in copies:
                copy.start()
            held[blank] = jnp.zeros(held.shape[1:], BF16)
            for copy in copies:
                copy.wait()

        own_start = run_starts(count_ref, group)[len(ORDER) - 1]
        ends = [0]
        for sender in range(len(ORDER)):
            ends.append(ends[-1] + count_ref[sender, group])

        def own_unit(unit):
            at = 0
            for c, (first, chunk) in enumerate(chunks):
                units = chunk[0].shape[0]
                base = firsts[len(received) + c * devices]
                inside = unit - 2 * first
                owner = lax.div(inside, units)
                spot = base + (owner ^ me) * units + inside - owner * units
                at = spot if c == 0 else jnp.where(inside >= 0, spot, at)
            return at

        planes_here = pl.ds(pl.multiple_of(pl.program_id(0) * 2 * step, 2 * step), 2 * step)
        for row in range(rows_dev):
            sender, slot = 0, row
            for g in range(1, len(ORDER)):
                later = row >= ends[g]
                sender = jnp.where(later, g, sender)
                slot = jnp.where(later, row - ends[g], slot)
            flip = sender ^ group
            window = jnp.where(flip == 1, 2, flip - 2)
            for half in range(2):
                at = jnp.where(flip == 0, own_unit(2 * (own_start + slot) + half), 2 * SLOT * window + 2 * slot + half)
                at = jnp.where(row < ends[-1], at, blank)
                for field in range(3):
                    block = held[at, field, planes_here].astype(F32).reshape(step, 2, lanes)
                    column = row * width + half * lanes
                    out_ref[:, field, :, column : column + lanes] = block

    return pl.pallas_call(
        body,
        grid_spec=pltpu.PrefetchScalarGridSpec(
            num_scalar_prefetch=2,
            grid=(planes // step,),
            in_specs=[hbm_spec()] * len(buffers),
            out_specs=pl.BlockSpec((step, 3, 2, rows_dev * width), lambda i, *_: (i, 0, 0, 0)),
            scratch_shapes=[
                pltpu.VMEM((blank + 1, 3, depth, lanes), BF16),
                pltpu.SemaphoreType.DMA((len(buffers),)),
            ],
        ),
        out_shape=jax.ShapeDtypeStruct((planes, 3, 2, rows_dev * width), F32),
        compiler_params=PARAMS,
        cost_estimate=pl.CostEstimate(
            flops=0, bytes_accessed=rows_dev * 36 * planes * width, transcendentals=0
        ),
    )(me, count, *buffers)


def exchange(buffers):
    devices = len(buffers)
    out = list(buffers)
    for s in reversed(range(1, devices)):
        out[s] = lax.ppermute(buffers[s], "gz", [(d, d ^ s) for d in range(devices)])
    return out


def run(rows, tables, fields, wall_operator, matrix, factors):
    devices, groups = lax.axis_size("gz"), lax.axis_size("ky")
    width = wall_operator.shape[0]
    rows_dev = fields.shape[3] // width
    me, _, count = tables
    chunks = []
    for first, size in ((0, 2 * SLOT), (2 * SLOT, rows - 2 * SLOT)):
        pencil = exchange(wall_rows(first, size, devices, tables, fields, wall_operator))
        chunks.append((first, exchange(transform(me, pencil, matrix, factors))))
    ready = windows((0, 1), me, count, chunks[:1]) + windows((2,), me, count, chunks)
    received = [
        lax.ppermute(window, "ky", [(g, g ^ flip) for g in range(groups)])
        for window, flip in zip(ready, ORDER)
    ]
    return place_rows(me, count, received, chunks, rows_dev, width)


def per_device(fields, wall_operator, remap_offset, remap_count):
    half_z = fields.shape[0] * lax.axis_size("gz") // 2
    matrix = jnp.asarray(mode_matrix(half_z))
    factors = jnp.asarray(mode_factors(half_z))
    rows_dev = fields.shape[3] // wall_operator.shape[0]
    me = jnp.stack([lax.axis_index("gz"), lax.axis_index("ky")]).astype(jnp.int32)
    tables = (me, remap_offset, remap_count)
    return run(rows_dev, tables, fields, wall_operator, matrix, factors)


def solution(mesh):
    placed = (P("gz", None, None, "ky"), P(), P(), P())
    return jax.shard_map(
        per_device, mesh=mesh, in_specs=placed, out_specs=P("gz", None, None, "ky"), check_vma=False
    )
```

```python
import functools
import math

import jax
import jax.numpy as jnp
import ml_dtypes
import numpy as np
from jax import lax
from jax.experimental import pallas as pl
from jax.experimental.pallas import tpu as pltpu
from jax.sharding import PartitionSpec as P

NU_COEF = 0.05
STEP_DT = 0.3
SLOT = 8
LANES = 128
ORDER = (2, 3, 1, 0)
BF16 = jnp.bfloat16
F32 = jnp.float32
PARAMS = pltpu.CompilerParams(vmem_limit_bytes=56 * 2**20)


def mode_matrix(half_z):
    row = np.arange(half_z)[:, None]
    column = np.arange(half_z)[None, :]
    norm = math.sqrt(2.0 / half_z)
    step = math.pi / (2 * half_z)
    cosine = norm * np.cos(((row * (2 * column + 1)) % (4 * half_z)) * step)
    sine = norm * np.sin((((row + 1) * (2 * (half_z - 1 - column) + 1)) % (4 * half_z)) * step)
    cosine = cosine.astype(np.float32).astype(ml_dtypes.bfloat16).astype(np.float32)
    sine = sine.astype(np.float32).astype(ml_dtypes.bfloat16).astype(np.float32)
    top = np.concatenate([0.5 * cosine, 0.5 * cosine[:, ::-1]], axis=1)
    bottom = np.concatenate([0.5 * sine[:, ::-1], -0.5 * sine], axis=1)
    whole = np.concatenate([top, bottom], axis=0)
    return np.kron(whole, np.eye(2, dtype=np.float32)).astype(ml_dtypes.bfloat16)


def mode_factors(half_z):
    index = np.arange(2 * half_z)
    wave = np.where(index < half_z, index, index - half_z + 1) * (math.pi / half_z)
    pair = np.stack([np.exp(-NU_COEF * wave * wave), STEP_DT * wave]).astype(np.float32)
    return np.broadcast_to(np.repeat(pair, 2, axis=1)[:, :, None], (2, 4 * half_z, LANES)).copy()


def run_starts(count_ref, group):
    starts = [0]
    for flip in ORDER:
        starts.append(starts[-1] + count_ref[group, group ^ flip])
    return starts


def hbm_spec():
    return pl.BlockSpec(memory_space=pl.ANY)


def whole_spec(shape):
    return pl.BlockSpec(shape, lambda *_: (0,) * len(shape))


def wall_rows(first, rows, devices, joined, tables, fields, wall_operator):
    width = wall_operator.shape[0]
    planes = fields.shape[0]
    depth = 2 * planes
    units = 2 * rows // devices
    strip = 3 * depth

    def body(me_ref, offset_ref, count_ref, fields_ref, wall_ref, *refs):
        outs, held = refs[:-1], refs[-1]
        me, group = me_ref[0], me_ref[1]
        starts = run_starts(count_ref, group)

        def source(i):
            row = 0
            for j, flip in enumerate(ORDER):
                here = offset_ref[group, group ^ flip] + i - starts[j]
                row = jnp.where((i >= starts[j]) & (i < starts[j + 1]), here, row)
            return row

        for s in range(0, devices, 2):
            for u in range(units):
                row = source(first + u * (devices // 2) + lax.shift_right_logical(me ^ s, 1))
                column = pl.multiple_of(row * width, width)
                for field in range(3):
                    at = u * strip + field * depth
                    held[at : at + depth] = fields_ref[:, field, :, pl.ds(column, width)].reshape(depth, width)
            walled = jnp.dot(held[...], wall_ref[...], preferred_element_type=F32).astype(BF16)
            halves = walled[:, :LANES], walled[:, LANES:]
            swapped = (me & 1) == 1
            for t in range(2):
                block = jnp.where(swapped, halves[1 - t], halves[t])
                for u in range(units):
                    for field in range(3):
                        at = u * strip + field * depth
                        if joined:
                            outs[0][me ^ (s + t), u, field] = block[at : at + depth]
                        else:
                            outs[s + t][u, field] = block[at : at + depth]

    shape = (units, 3, depth, LANES)
    shapes = [(devices,) + shape] if joined else [shape] * devices
    return pl.pallas_call(
        body,
        grid_spec=pltpu.PrefetchScalarGridSpec(
            num_scalar_prefetch=3,
            grid=(1,),
            in_specs=[whole_spec(fields.shape), whole_spec(wall_operator.shape)],
            out_specs=[whole_spec(shape) for shape in shapes],
            scratch_shapes=[pltpu.VMEM((units * strip, width), BF16)],
        ),
        out_shape=[jax.ShapeDtypeStruct(shape, BF16) for shape in shapes],
        compiler_params=PARAMS,
        cost_estimate=pl.CostEstimate(
            flops=rows * 12 * planes * width * width, bytes_accessed=12 * planes * width * (rows + 32), transcendentals=0
        ),
    )(*tables, fields, wall_operator)


def transform(me, pencil, begin, units, devices, joined_out, matrix, factors):
    joined = len(pencil) == 1
    held, _, depth, lanes = pencil[0].shape[-4:]
    part, skip = divmod(begin, units)
    if skip:
        part, skip = 0, begin
    size = devices * depth
    strip = 3 * lanes

    def body(me_ref, *refs):
        ins, (matrix_ref, factors_ref) = refs[: len(pencil)], refs[len(pencil) : len(pencil) + 2]
        outs, (block, turned, scale) = refs[len(pencil) + 2 : -3], refs[-3:]
        for s in range(devices):
            at = pl.ds(pl.multiple_of((me_ref[0] ^ s) * depth, depth), depth)
            if not joined_out:
                turned[s * depth : (s + 1) * depth] = matrix_ref[at]
                for k in range(2):
                    scale[k, s * depth : (s + 1) * depth] = factors_ref[k, at]
            to = slice(s * depth, (s + 1) * depth) if joined else at
            for u in range(units):
                for f in range(3):
                    column = u * strip + f * lanes
                    block[to, column : column + lanes] = ins[0][s, skip + u, f] if joined else ins[s][skip + u, f]
        table, scales = (matrix_ref, factors_ref) if joined_out else (turned, scale)
        for u in range(units):
            modes = jnp.dot(table[...], block[:, u * strip : (u + 1) * strip], preferred_element_type=F32)
            velocity, buoyant, magnetic = (modes[:, f * lanes : f * lanes + lanes] for f in range(3))
            damping, wave = scales[0], scales[1]
            coupled = (
                damping * (velocity + STEP_DT * buoyant + wave * magnetic),
                damping * (buoyant - STEP_DT * velocity),
                damping * (magnetic - wave * velocity),
            )
            for f in range(3):
                rounded = coupled[f].astype(BF16)
                for s in range(devices):
                    if joined_out:
                        outs[0][s, u, f] = rounded[s * depth : (s + 1) * depth]
                    else:
                        outs[s][u, f] = rounded[s * depth : (s + 1) * depth]

    shape = (units, 3, depth, lanes)
    shapes = [(devices,) + shape] if joined_out else [shape] * devices
    taken = (held if skip else units, 3, depth, lanes)
    if joined:
        specs = [pl.BlockSpec((devices,) + taken, lambda *_: (0, part, 0, 0, 0))]
    else:
        specs = [pl.BlockSpec(taken, lambda *_: (part, 0, 0, 0))] * devices
    return pl.pallas_call(
        body,
        grid_spec=pltpu.PrefetchScalarGridSpec(
            num_scalar_prefetch=1,
            grid=(1,),
            in_specs=specs + [whole_spec(matrix.shape), whole_spec(factors.shape)],
            out_specs=[whole_spec(shape) for shape in shapes],
            scratch_shapes=[
                pltpu.VMEM((size, units * strip), BF16),
                pltpu.VMEM((size, size), BF16),
                pltpu.VMEM((2, size, lanes), F32),
            ],
        ),
        out_shape=[jax.ShapeDtypeStruct(shape, BF16) for shape in shapes],
        compiler_params=PARAMS,
        cost_estimate=pl.CostEstimate(
            flops=units * 6 * size * size * lanes, bytes_accessed=units * 12 * size * lanes, transcendentals=0
        ),
    )(me, *pencil, matrix, factors)


def held_unit(me, pieces, unit):
    at, base = 0, 0
    for c, (first, buffers) in enumerate(pieces):
        if len(buffers) == 1:
            (devices, units), flip = buffers[0].shape[:2], 0
        else:
            (devices, units), flip = (len(buffers), buffers[0].shape[0]), me
        inside = unit - 2 * first
        spot = base + (lax.rem(inside, devices) ^ flip) * units + lax.div(inside, devices)
        at = spot if c == 0 else jnp.where(inside >= 0, spot, at)
        base += devices * units
    return at


def bring(buffers, held, sem):
    copies, first = [], 0
    for b, buffer in enumerate(buffers):
        size = buffer.shape[0]
        copies.append(pltpu.make_async_copy(buffer, held.at[pl.ds(first, size)], sem.at[b]))
        first += size
    for copy in copies:
        copy.start()
    return copies


def windows(which, me, count, pieces):
    buffers = [b.reshape((-1,) + b.shape[-3:]) for _, piece in pieces for b in piece]
    total = sum(b.shape[0] for b in buffers)
    shape = (2 * SLOT,) + buffers[0].shape[1:]

    def body(me_ref, count_ref, *refs):
        ins, outs, (held, sem) = refs[: len(buffers)], refs[len(buffers) : -2], refs[-2:]
        copies = bring(ins, held, sem)
        starts = run_starts(count_ref, me_ref[1])
        for copy in copies:
            copy.wait()
        for o, j in enumerate(which):
            for slot in range(2 * SLOT):
                unit = jnp.minimum(2 * starts[j] + slot, total - 1)
                outs[o][slot] = held[held_unit(me_ref[0], pieces, unit)]

    return pl.pallas_call(
        body,
        grid_spec=pltpu.PrefetchScalarGridSpec(
            num_scalar_prefetch=2,
            grid=(1,),
            in_specs=[hbm_spec()] * len(buffers),
            out_specs=[whole_spec(shape)] * len(which),
            scratch_shapes=[
                pltpu.VMEM((total,) + buffers[0].shape[1:], BF16),
                pltpu.SemaphoreType.DMA((len(buffers),)),
            ],
        ),
        out_shape=[jax.ShapeDtypeStruct(shape, BF16)] * len(which),
        compiler_params=PARAMS,
        cost_estimate=pl.CostEstimate(flops=0, bytes_accessed=2**21 * len(which), transcendentals=0),
    )(me, count, *buffers)


def place_rows(me, count, held, rows_dev, width):
    _, _, depth, lanes = held[0].shape
    planes, step = depth // 2, 8

    def body(me_ref, count_ref, *refs):
        ins, out_ref, (held, sem) = refs[: len(ORDER)], refs[len(ORDER)], refs[-2:]
        group = me_ref[1]
        blank = 2 * SLOT * len(ORDER)

        @pl.when(pl.program_id(0) == 0)
        def _():
            copies = bring(ins, held, sem)
            held[blank] = jnp.zeros(held.shape[1:], BF16)
            for copy in copies:
                copy.wait()

        ends = [0]
        for sender in range(len(ORDER)):
            ends.append(ends[-1] + count_ref[sender, group])

        here = pl.ds(pl.multiple_of(pl.program_id(0) * 2 * step, 2 * step), 2 * step)
        for row in range(rows_dev):
            sender, slot = 0, row
            for g in range(1, len(ORDER)):
                later = row >= ends[g]
                sender = jnp.where(later, g, sender)
                slot = jnp.where(later, row - ends[g], slot)
            window = 0
            for j, flip in enumerate(ORDER):
                window = jnp.where((sender ^ group) == flip, j, window)
            for half in range(2):
                at = jnp.where(row < ends[-1], 2 * SLOT * window + 2 * slot + half, blank)
                column = row * width + half * lanes
                for field in range(3):
                    block = held[at, field, here].astype(F32).reshape(step, 2, lanes)
                    out_ref[:, field, :, column : column + lanes] = block

    return pl.pallas_call(
        body,
        grid_spec=pltpu.PrefetchScalarGridSpec(
            num_scalar_prefetch=2,
            grid=(planes // step,),
            in_specs=[hbm_spec()] * len(ORDER),
            out_specs=pl.BlockSpec((step, 3, 2, rows_dev * width), lambda i, *_: (i, 0, 0, 0)),
            scratch_shapes=[
                pltpu.VMEM((2 * SLOT * len(ORDER) + 1, 3, depth, lanes), BF16),
                pltpu.SemaphoreType.DMA((len(ORDER),)),
            ],
        ),
        out_shape=jax.ShapeDtypeStruct((planes, 3, 2, rows_dev * width), F32),
        compiler_params=PARAMS,
        cost_estimate=pl.CostEstimate(
            flops=0, bytes_accessed=rows_dev * 36 * planes * width, transcendentals=0
        ),
    )(me, count, *held)


def exchange(buffers, devices):
    if len(buffers) == 1:
        return [lax.all_to_all(buffers[0], "gz", split_axis=0, concat_axis=0, tiled=True)]
    out = list(buffers)
    for s in reversed(range(1, devices)):
        out[s] = lax.ppermute(buffers[s], "gz", [(d, d ^ s) for d in range(devices)])
    return out


def after(values, earlier):
    return list(lax.optimization_barrier((tuple(values), earlier))[0])


def run(plan, tables, fields, wall_operator, matrix, factors):
    devices, groups = lax.axis_size("gz"), lax.axis_size("ky")
    me, _, count = tables
    waves, first = [], 0
    for joined, parts in plan:
        walled = wall_rows(first, sum(part for part, _ in parts), devices, joined, tables, fields, wall_operator)
        pencil, begin = exchange(walled, devices), 0
        for part, joined_out in parts:
            waves.append((first, pencil, begin, 2 * part // devices, joined_out))
            first += part
            begin += 2 * part // devices
    pieces, sent = [], []

    def send_window():
        j = len(sent)
        needed = [piece for piece in pieces if piece[0] < SLOT * (j + 1)]
        if sent:
            first, last = needed[-1]
            needed[-1] = (first, after(last, tuple(sent)))
        window, *own = windows((j, j + 1) if j == len(ORDER) - 2 else (j,), me, count, needed)
        pairs = [(g, g ^ ORDER[j]) for g in range(groups)]
        sent.append(lax.ppermute(window, "ky", pairs))
        return window, own

    for first, pencil, begin, units, joined_out in waves:
        modes = list(transform(me, pencil, begin, units, devices, joined_out, matrix, factors))
        if HOLD and first == waves[-1][0] and first >= SLOT:
            window, _ = send_window()
            modes = after(modes, window)
        pieces.append((first, exchange(modes, devices)))
    while len(sent) < len(ORDER) - 1:
        _, own = send_window()
    return tuple(sent + own)


HOLD = True


def plans(devices, rows_dev):
    if devices != 8:
        grain = devices // 2
        return [[(False, [(grain, False)])] * (rows_dev // grain)]
    return [PLAN(rows) for rows in range(2 * SLOT + 4, rows_dev + 1, 4)]


def PLAN(rows):
    return [(False, [(8, True), (8, True), (rows - 16, True)])]


def per_device(fields, wall_operator, remap_offset, remap_count):
    devices = lax.axis_size("gz")
    half_z = fields.shape[0] * devices // 2
    matrix = jnp.asarray(mode_matrix(half_z))
    factors = jnp.asarray(mode_factors(half_z))
    width = wall_operator.shape[0]
    rows_dev = fields.shape[3] // width
    me = jnp.stack([lax.axis_index("gz"), lax.axis_index("ky")]).astype(jnp.int32)
    tables = (me, remap_offset, remap_count)
    chosen = plans(devices, rows_dev)
    most = jnp.max(jnp.sum(remap_count, axis=1))
    choice = jnp.int32(0)
    for plan in chosen[:-1]:
        choice += (most > sum(part for _, parts in plan for part, _ in parts)).astype(jnp.int32)
    branches = [functools.partial(run, plan) for plan in chosen]
    held = lax.switch(choice, branches, tables, fields, wall_operator, matrix, factors)
    return place_rows(me, remap_count, held, rows_dev, width)


def solution(mesh):
    placed = (P("gz", None, None, "ky"), P(), P(), P())
    return jax.shard_map(
        per_device, mesh=mesh, in_specs=placed, out_specs=P("gz", None, None, "ky"), check_vma=False
    )
```

```python
import functools
import math

import jax
import jax.numpy as jnp
import ml_dtypes
import numpy as np
from jax import lax
from jax.experimental import pallas as pl
from jax.experimental.pallas import tpu as pltpu
from jax.sharding import PartitionSpec as P

NU_COEF = 0.05
STEP_DT = 0.3
SLOT = 8
LANES = 128
FLIPS = (2, 0)
SENDERS = (0, 2, 1, 3)
BF16 = jnp.bfloat16
F32 = jnp.float32
PARAMS = pltpu.CompilerParams(vmem_limit_bytes=56 * 2**20)


def mode_matrix(half_z):
    row = np.arange(half_z)[:, None]
    column = np.arange(half_z)[None, :]
    norm = math.sqrt(2.0 / half_z)
    step = math.pi / (2 * half_z)
    cosine = norm * np.cos(((row * (2 * column + 1)) % (4 * half_z)) * step)
    sine = norm * np.sin((((row + 1) * (2 * (half_z - 1 - column) + 1)) % (4 * half_z)) * step)
    cosine = cosine.astype(np.float32).astype(ml_dtypes.bfloat16).astype(np.float32)
    sine = sine.astype(np.float32).astype(ml_dtypes.bfloat16).astype(np.float32)
    top = np.concatenate([0.5 * cosine, 0.5 * cosine[:, ::-1]], axis=1)
    bottom = np.concatenate([0.5 * sine[:, ::-1], -0.5 * sine], axis=1)
    whole = np.concatenate([top, bottom], axis=0)
    return np.kron(whole, np.eye(2, dtype=np.float32)).astype(ml_dtypes.bfloat16)


def mode_factors(half_z):
    index = np.arange(2 * half_z)
    wave = np.where(index < half_z, index, index - half_z + 1) * (math.pi / half_z)
    pair = np.stack([np.exp(-NU_COEF * wave * wave), STEP_DT * wave]).astype(np.float32)
    return np.broadcast_to(np.repeat(pair, 2, axis=1)[:, :, None], (2, 4 * half_z, LANES)).copy()


def sent_runs(count, group, flip):
    first = count[group, group ^ flip]
    return first, first + count[group, group ^ flip ^ 1]


def choose(count, sizes):
    def body(count_ref, out_ref):
        for k, flip in enumerate(FLIPS):
            most = 0
            for group in range(4):
                most = jnp.maximum(most, sent_runs(count_ref, group, flip)[1])
            out_ref[k] = sum((most > size).astype(jnp.int32) for size in sizes[:-1])

    smem = pl.BlockSpec(memory_space=pltpu.SMEM)
    return pl.pallas_call(
        body, in_specs=[smem], out_specs=smem, out_shape=jax.ShapeDtypeStruct((2,), jnp.int32)
    )(count)


def hbm_spec():
    return pl.BlockSpec(memory_space=pl.ANY)


def whole_spec(shape):
    return pl.BlockSpec(shape, lambda *_: (0,) * len(shape))


def wall_rows(flip, rows, devices, tables, fields, wall_operator):
    width = wall_operator.shape[0]
    planes = fields.shape[0]
    depth = 2 * planes
    units = 2 * rows // devices
    strip = 3 * depth

    def body(me_ref, offset_ref, count_ref, fields_ref, wall_ref, *refs):
        outs, held = refs[:-1], refs[-1]
        me, group = me_ref[0], me_ref[1]
        middle, end = sent_runs(count_ref, group, flip)
        begins = offset_ref[group, group ^ flip], offset_ref[group, group ^ flip ^ 1] - middle

        def source(i):
            return jnp.where(i < end, i + jnp.where(i < middle, begins[0], begins[1]), 0)

        for s in range(0, devices, 2):
            for u in range(units):
                row = source(u * (devices // 2) + lax.shift_right_logical(me ^ s, 1))
                column = pl.multiple_of(row * width, width)
                for field in range(3):
                    at = u * strip + field * depth
                    held[at : at + depth] = fields_ref[:, field, :, pl.ds(column, width)].reshape(depth, width)
            walled = jnp.dot(held[...], wall_ref[...], preferred_element_type=F32).astype(BF16)
            halves = walled[:, :LANES], walled[:, LANES:]
            swapped = (me & 1) == 1
            for t in range(2):
                block = jnp.where(swapped, halves[1 - t], halves[t])
                for u in range(units):
                    for field in range(3):
                        at = u * strip + field * depth
                        outs[s + t][u, field] = block[at : at + depth]

    shape = (units, 3, depth, LANES)
    return pl.pallas_call(
        body,
        grid_spec=pltpu.PrefetchScalarGridSpec(
            num_scalar_prefetch=3,
            grid=(1,),
            in_specs=[whole_spec(fields.shape), whole_spec(wall_operator.shape)],
            out_specs=[whole_spec(shape)] * devices,
            scratch_shapes=[pltpu.VMEM((units * strip, width), BF16)],
        ),
        out_shape=[jax.ShapeDtypeStruct(shape, BF16)] * devices,
        compiler_params=PARAMS,
        cost_estimate=pl.CostEstimate(
            flops=rows * 12 * planes * width * width, bytes_accessed=12 * planes * width * (rows + 32), transcendentals=0
        ),
    )(*tables, fields, wall_operator)


def transform(me, pencil, matrix, factors):
    devices = len(pencil)
    units, _, depth, lanes = pencil[0].shape
    size = devices * depth
    strip = 3 * lanes

    def body(me_ref, *refs):
        ins, (matrix_ref, factors_ref) = refs[:devices], refs[devices : devices + 2]
        outs, (block, turned, scale) = refs[devices + 2 : -3], refs[-3:]
        for s in range(devices):
            at = pl.ds(pl.multiple_of((me_ref[0] ^ s) * depth, depth), depth)
            turned[s * depth : (s + 1) * depth] = matrix_ref[at]
            for k in range(2):
                scale[k, s * depth : (s + 1) * depth] = factors_ref[k, at]
            for u in range(units):
                for f in range(3):
                    column = u * strip + f * lanes
                    block[at, column : column + lanes] = ins[s][u, f]
        for u in range(units):
            modes = jnp.dot(turned[...], block[:, u * strip : (u + 1) * strip], preferred_element_type=F32)
            velocity, buoyant, magnetic = (modes[:, f * lanes : f * lanes + lanes] for f in range(3))
            damping, wave = scale[0], scale[1]
            coupled = (
                damping * (velocity + STEP_DT * buoyant + wave * magnetic),
                damping * (buoyant - STEP_DT * velocity),
                damping * (magnetic - wave * velocity),
            )
            for f in range(3):
                rounded = coupled[f].astype(BF16)
                for s in range(devices):
                    outs[s][u, f] = rounded[s * depth : (s + 1) * depth]

    spec = whole_spec(pencil[0].shape)
    return pl.pallas_call(
        body,
        grid_spec=pltpu.PrefetchScalarGridSpec(
            num_scalar_prefetch=1,
            grid=(1,),
            in_specs=[spec] * devices + [whole_spec(matrix.shape), whole_spec(factors.shape)],
            out_specs=[spec] * devices,
            scratch_shapes=[
                pltpu.VMEM((size, units * strip), BF16),
                pltpu.VMEM((size, size), BF16),
                pltpu.VMEM((2, size, lanes), F32),
            ],
        ),
        out_shape=[jax.ShapeDtypeStruct(pencil[0].shape, BF16)] * devices,
        compiler_params=PARAMS,
        cost_estimate=pl.CostEstimate(
            flops=units * 6 * size * size * lanes, bytes_accessed=units * 12 * size * lanes, transcendentals=0
        ),
    )(me, *pencil, matrix, factors)


def held_unit(me, pieces, unit):
    at, base = 0, 0
    for c, (first, buffers) in enumerate(pieces):
        devices, units = len(buffers), buffers[0].shape[0]
        inside = unit - 2 * first
        spot = base + (lax.rem(inside, devices) ^ me) * units + lax.div(inside, devices)
        at = spot if c == 0 else jnp.where(inside >= 0, spot, at)
        base += devices * units
    return at


def bring(buffers, held, sem):
    copies, first = [], 0
    for b, buffer in enumerate(buffers):
        size = buffer.shape[0]
        copies.append(pltpu.make_async_copy(buffer, held.at[pl.ds(first, size)], sem.at[b]))
        first += size
    for copy in copies:
        copy.start()
    return copies


def windows(me, count, pieces):
    buffers = [b for _, piece in pieces for b in piece]
    total = sum(b.shape[0] for b in buffers)
    unit_shape = buffers[0].shape[1:]
    shape = (2 * SLOT,) + unit_shape

    def body(me_ref, count_ref, *refs):
        ins, outs, (held, sem) = refs[: len(buffers)], refs[len(buffers) : -2], refs[-2:]
        copies = bring(ins, held, sem)
        group = me_ref[1]
        far = 2 * sent_runs(count_ref, group ^ 2, 2)[0]
        near = 2 * (pieces[1][0] + sent_runs(count_ref, group, 0)[0])
        for copy in copies:
            copy.wait()
        for out, at, start in ((outs[0], 0, 2 * pieces[1][0]), (outs[1], 0, 0), (outs[2], 0, near), (outs[2], 2 * SLOT, far)):
            for slot in range(2 * SLOT):
                out[at + slot] = held[held_unit(me_ref[0], pieces, jnp.minimum(start + slot, total - 1))]

    shapes = [shape, shape, (4 * SLOT,) + unit_shape]
    return pl.pallas_call(
        body,
        grid_spec=pltpu.PrefetchScalarGridSpec(
            num_scalar_prefetch=2,
            grid=(1,),
            in_specs=[hbm_spec()] * len(buffers),
            out_specs=[whole_spec(shape) for shape in shapes],
            scratch_shapes=[pltpu.VMEM((total,) + unit_shape, BF16), pltpu.SemaphoreType.DMA((len(buffers),))],
        ),
        out_shape=[jax.ShapeDtypeStruct(shape, BF16) for shape in shapes],
        compiler_params=PARAMS,
        cost_estimate=pl.CostEstimate(flops=0, bytes_accessed=2**23, transcendentals=0),
    )(me, count, *buffers)


def place_rows(me, count, held, rows_dev, width):
    _, _, depth, lanes = held[0].shape
    planes, step = depth // 2, 8

    def body(me_ref, count_ref, *refs):
        ins, out_ref, (held, sem) = refs[:-3], refs[-3], refs[-2:]
        group = me_ref[1]
        blank = 2 * SLOT * len(SENDERS)

        @pl.when(pl.program_id(0) == 0)
        def _():
            copies = bring(ins, held, sem)
            held[blank] = jnp.zeros(held.shape[1:], BF16)
            for copy in copies:
                copy.wait()

        ends = [0]
        for sender in range(len(SENDERS)):
            ends.append(ends[-1] + count_ref[sender, group])

        here = pl.ds(pl.multiple_of(pl.program_id(0) * 2 * step, 2 * step), 2 * step)
        for row in range(rows_dev):
            sender, slot = 0, row
            for g in range(1, len(SENDERS)):
                later = row >= ends[g]
                sender = jnp.where(later, g, sender)
                slot = jnp.where(later, row - ends[g], slot)
            window = 0
            for j, flip in enumerate(SENDERS):
                window = jnp.where((sender ^ group) == flip, j, window)
            for half in range(2):
                at = jnp.where(row < ends[-1], 2 * SLOT * window + 2 * slot + half, blank)
                column = row * width + half * lanes
                for field in range(3):
                    block = held[at, field, here].astype(F32).reshape(step, 2, lanes)
                    out_ref[:, field, :, column : column + lanes] = block

    return pl.pallas_call(
        body,
        grid_spec=pltpu.PrefetchScalarGridSpec(
            num_scalar_prefetch=2,
            grid=(planes // step,),
            in_specs=[hbm_spec()] * len(held),
            out_specs=pl.BlockSpec((step, 3, 2, rows_dev * width), lambda i, *_: (i, 0, 0, 0)),
            scratch_shapes=[
                pltpu.VMEM((2 * SLOT * len(SENDERS) + 1, 3, depth, lanes), BF16),
                pltpu.SemaphoreType.DMA((len(held),)),
            ],
        ),
        out_shape=jax.ShapeDtypeStruct((planes, 3, 2, rows_dev * width), F32),
        compiler_params=PARAMS,
        cost_estimate=pl.CostEstimate(
            flops=0, bytes_accessed=rows_dev * 36 * planes * width, transcendentals=0
        ),
    )(me, count, *held)


def permute(value, s, flip):
    devices, groups = lax.axis_size("gz"), lax.axis_size("ky")
    pairs = [(d * groups + g, (d ^ s) * groups + (g ^ flip)) for d in range(devices) for g in range(groups)]
    return lax.ppermute(value, ("gz", "ky"), pairs)


def exchange(buffers, flip):
    out = list(buffers)
    for s in reversed(range(0 if flip else 1, len(buffers))):
        out[s] = permute(buffers[s], s, flip)
    return out


def run(sizes, tables, fields, wall_operator, matrix, factors):
    devices = lax.axis_size("gz")
    me, _, count = tables
    pencils = [
        exchange(wall_rows(flip, rows, devices, tables, fields, wall_operator), flip)
        for flip, rows in zip(FLIPS, sizes)
    ]
    modes = [exchange(transform(me, pencil, matrix, factors), 0) for pencil in pencils]
    mine, theirs, sent = windows(me, count, [(0, modes[0]), (sizes[0], modes[1])])
    return mine, theirs, permute(sent, 0, 1)


def per_device(fields, wall_operator, remap_offset, remap_count):
    devices = lax.axis_size("gz")
    half_z = fields.shape[0] * devices // 2
    matrix = jnp.asarray(mode_matrix(half_z))
    factors = jnp.asarray(mode_factors(half_z))
    width = wall_operator.shape[0]
    rows_dev = fields.shape[3] // width
    me = jnp.stack([lax.axis_index("gz"), lax.axis_index("ky")]).astype(jnp.int32)
    tables = (me, remap_offset, remap_count)
    sizes = [size for size in (12, 16) if 2 * size % devices == 0]
    branches = [functools.partial(run, (far, near)) for far in sizes for near in sizes]
    arguments = (tables, fields, wall_operator, matrix, factors)
    if len(branches) == 1:
        held = branches[0](*arguments)
    else:
        choice = choose(remap_count, sizes)
        held = lax.switch(len(sizes) * choice[0] + choice[1], branches, *arguments)
    return place_rows(me, remap_count, held, rows_dev, width)


def solution(mesh):
    placed = (P("gz", None, None, "ky"), P(), P(), P())
    return jax.shard_map(
        per_device, mesh=mesh, in_specs=placed, out_specs=P("gz", None, None, "ky"), check_vma=False
    )
```

```python
import functools
import math

import jax
import jax.numpy as jnp
import ml_dtypes
import numpy as np
from jax import lax
from jax.experimental import pallas as pl
from jax.experimental.pallas import tpu as pltpu
from jax.sharding import PartitionSpec as P

NU_COEF = 0.05
STEP_DT = 0.3
SLOT = 8
LANES = 128
FLIPS = (2, 0)
SENDERS = (0, 2, 1, 3)
BF16 = jnp.bfloat16
F32 = jnp.float32
PARAMS = pltpu.CompilerParams(vmem_limit_bytes=56 * 2**20)


def mode_matrix(half_z):
    row = np.arange(half_z)[:, None]
    column = np.arange(half_z)[None, :]
    norm = math.sqrt(2.0 / half_z)
    step = math.pi / (2 * half_z)
    cosine = norm * np.cos(((row * (2 * column + 1)) % (4 * half_z)) * step)
    sine = norm * np.sin((((row + 1) * (2 * (half_z - 1 - column) + 1)) % (4 * half_z)) * step)
    cosine = cosine.astype(np.float32).astype(ml_dtypes.bfloat16).astype(np.float32)
    sine = sine.astype(np.float32).astype(ml_dtypes.bfloat16).astype(np.float32)
    top = np.concatenate([0.5 * cosine, 0.5 * cosine[:, ::-1]], axis=1)
    bottom = np.concatenate([0.5 * sine[:, ::-1], -0.5 * sine], axis=1)
    whole = np.concatenate([top, bottom], axis=0)
    return np.kron(whole, np.eye(2, dtype=np.float32)).astype(ml_dtypes.bfloat16)


def mode_factors(half_z):
    index = np.arange(2 * half_z)
    wave = np.where(index < half_z, index, index - half_z + 1) * (math.pi / half_z)
    pair = np.stack([np.exp(-NU_COEF * wave * wave), STEP_DT * wave]).astype(np.float32)
    return np.broadcast_to(np.repeat(pair, 2, axis=1)[:, :, None], (2, 4 * half_z, LANES)).copy()


def sent_runs(count, group, flip):
    first = count[group, group ^ flip]
    return first, first + count[group, group ^ flip ^ 1]


def choose(count, sizes):
    def body(count_ref, out_ref):
        choice = 0
        for flip in FLIPS:
            most = 0
            for group in range(4):
                most = jnp.maximum(most, sent_runs(count_ref, group, flip)[1])
            choice = choice * len(sizes) + sum((most > size).astype(jnp.int32) for size in sizes[:-1])
        out_ref[0] = choice

    smem = pl.BlockSpec(memory_space=pltpu.SMEM)
    return pl.pallas_call(
        body, in_specs=[smem], out_specs=smem, out_shape=jax.ShapeDtypeStruct((1,), jnp.int32)
    )(count)[0]


def hbm_spec():
    return pl.BlockSpec(memory_space=pl.ANY)


def whole_spec(shape):
    return pl.BlockSpec(shape, lambda *_: (0,) * len(shape))


def wall_rows(flip, rows, devices, tables, fields, wall_operator):
    width = wall_operator.shape[0]
    planes = fields.shape[0]
    depth = 2 * planes
    units = 2 * rows // devices
    strip = 3 * depth

    def body(me_ref, offset_ref, count_ref, fields_ref, wall_ref, *refs):
        outs, held = refs[:-1], refs[-1]
        me, group = me_ref[0], me_ref[1]
        middle, end = sent_runs(count_ref, group, flip)
        begins = offset_ref[group, group ^ flip], offset_ref[group, group ^ flip ^ 1] - middle

        def source(i):
            return jnp.where(i < end, i + jnp.where(i < middle, begins[0], begins[1]), 0)

        for s in range(0, devices, 2):
            for u in range(units):
                row = source(u * (devices // 2) + lax.shift_right_logical(me ^ s, 1))
                column = pl.multiple_of(row * width, width)
                for field in range(3):
                    at = u * strip + field * depth
                    held[at : at + depth] = fields_ref[:, field, :, pl.ds(column, width)].reshape(depth, width)
            walled = jnp.dot(held[...], wall_ref[...], preferred_element_type=F32).astype(BF16)
            halves = walled[:, :LANES], walled[:, LANES:]
            swapped = (me & 1) == 1
            for t in range(2):
                block = jnp.where(swapped, halves[1 - t], halves[t])
                for u in range(units):
                    for field in range(3):
                        at = u * strip + field * depth
                        outs[s + t][u, field] = block[at : at + depth]

    shape = (units, 3, depth, LANES)
    return pl.pallas_call(
        body,
        grid_spec=pltpu.PrefetchScalarGridSpec(
            num_scalar_prefetch=3,
            grid=(1,),
            in_specs=[whole_spec(fields.shape), whole_spec(wall_operator.shape)],
            out_specs=[whole_spec(shape)] * devices,
            scratch_shapes=[pltpu.VMEM((units * strip, width), BF16)],
        ),
        out_shape=[jax.ShapeDtypeStruct(shape, BF16)] * devices,
        compiler_params=PARAMS,
        cost_estimate=pl.CostEstimate(
            flops=rows * 12 * planes * width * width, bytes_accessed=12 * planes * width * (rows + 32), transcendentals=0
        ),
    )(*tables, fields, wall_operator)


def transform(me, pencil, matrix, factors):
    devices = len(pencil)
    units, _, depth, lanes = pencil[0].shape
    size = devices * depth
    strip = 3 * lanes

    def body(me_ref, *refs):
        ins, (matrix_ref, factors_ref) = refs[:devices], refs[devices : devices + 2]
        outs, (block, turned, scale) = refs[devices + 2 : -3], refs[-3:]
        for s in range(devices):
            at = pl.ds(pl.multiple_of((me_ref[0] ^ s) * depth, depth), depth)
            turned[s * depth : (s + 1) * depth] = matrix_ref[at]
            for k in range(2):
                scale[k, s * depth : (s + 1) * depth] = factors_ref[k, at]
            for u in range(units):
                for f in range(3):
                    column = u * strip + f * lanes
                    block[at, column : column + lanes] = ins[s][u, f]
        for u in range(units):
            modes = jnp.dot(turned[...], block[:, u * strip : (u + 1) * strip], preferred_element_type=F32)
            velocity, buoyant, magnetic = (modes[:, f * lanes : f * lanes + lanes] for f in range(3))
            damping, wave = scale[0], scale[1]
            coupled = (
                damping * (velocity + STEP_DT * buoyant + wave * magnetic),
                damping * (buoyant - STEP_DT * velocity),
                damping * (magnetic - wave * velocity),
            )
            for f in range(3):
                rounded = coupled[f].astype(BF16)
                for s in range(devices):
                    outs[s][u, f] = rounded[s * depth : (s + 1) * depth]

    spec = whole_spec(pencil[0].shape)
    return pl.pallas_call(
        body,
        grid_spec=pltpu.PrefetchScalarGridSpec(
            num_scalar_prefetch=1,
            grid=(1,),
            in_specs=[spec] * devices + [whole_spec(matrix.shape), whole_spec(factors.shape)],
            out_specs=[spec] * devices,
            scratch_shapes=[
                pltpu.VMEM((size, units * strip), BF16),
                pltpu.VMEM((size, size), BF16),
                pltpu.VMEM((2, size, lanes), F32),
            ],
        ),
        out_shape=[jax.ShapeDtypeStruct(pencil[0].shape, BF16)] * devices,
        compiler_params=PARAMS,
        cost_estimate=pl.CostEstimate(
            flops=units * 6 * size * size * lanes, bytes_accessed=units * 12 * size * lanes, transcendentals=0
        ),
    )(me, *pencil, matrix, factors)


def bring(buffers, held, sem):
    copies, first = [], 0
    for b, buffer in enumerate(buffers):
        size = buffer.shape[0]
        copies.append(pltpu.make_async_copy(buffer, held.at[pl.ds(first, size)], sem.at[b]))
        first += size
    for copy in copies:
        copy.start()
    return copies


def windows(me, count, pieces, wanted):
    buffers = [b for _, piece in pieces for b in piece]
    sizes = [sum(b.shape[0] for b in piece) for _, piece in pieces]
    bases = {flip: sum(sizes[:p]) for p, (flip, _) in enumerate(pieces)}
    units = {flip: piece[0].shape[0] for flip, piece in pieces}
    devices = len(pieces[0][1])
    unit_shape = buffers[0].shape[1:]
    shape = (2 * SLOT,) + unit_shape

    def body(me_ref, count_ref, *refs):
        ins, outs, (held, sem) = refs[: len(buffers)], refs[len(buffers) : -2], refs[-2:]
        copies = bring(ins, held, sem)
        group = me_ref[1]
        starts = {(flip, 0): 0 for flip, _ in pieces}
        starts |= {(flip, 1): 2 * sent_runs(count_ref, group ^ flip, flip)[0] for flip, _ in pieces}
        for copy in copies:
            copy.wait()
        for out, (flip, to) in zip(outs, wanted):
            for slot in range(2 * SLOT):
                unit = jnp.minimum(starts[flip, to] + slot, devices * units[flip] - 1)
                owner = lax.rem(unit, devices) ^ me_ref[0]
                out[slot] = held[bases[flip] + owner * units[flip] + lax.div(unit, devices)]

    return pl.pallas_call(
        body,
        grid_spec=pltpu.PrefetchScalarGridSpec(
            num_scalar_prefetch=2,
            grid=(1,),
            in_specs=[hbm_spec()] * len(buffers),
            out_specs=[whole_spec(shape)] * len(wanted),
            scratch_shapes=[pltpu.VMEM((sum(sizes),) + unit_shape, BF16), pltpu.SemaphoreType.DMA((len(buffers),))],
        ),
        out_shape=[jax.ShapeDtypeStruct(shape, BF16)] * len(wanted),
        compiler_params=PARAMS,
        cost_estimate=pl.CostEstimate(flops=0, bytes_accessed=2**21 * len(wanted), transcendentals=0),
    )(me, count, *buffers)


def place_rows(me, count, held, rows_dev, width):
    _, _, depth, lanes = held[0].shape
    planes, step = depth // 2, 8

    def body(me_ref, count_ref, *refs):
        ins, out_ref, (held, sem) = refs[:-3], refs[-3], refs[-2:]
        group = me_ref[1]
        blank = 2 * SLOT * len(SENDERS)

        now = pl.program_id(0)

        def copies(i):
            planes_of = pl.ds(pl.multiple_of(i * 2 * step, 2 * step), 2 * step)
            return [
                pltpu.make_async_copy(
                    ref.at[:, :, planes_of], held.at[pl.ds(2 * SLOT * w, 2 * SLOT), :, planes_of], sem.at[i, w]
                )
                for w, ref in enumerate(ins)
            ]

        @pl.when(now == 0)
        def _():
            for i in range(planes // step):
                for copy in copies(i):
                    copy.start()
            held[blank] = jnp.zeros(held.shape[1:], BF16)

        for copy in copies(now):
            copy.wait()

        ends = [0]
        for sender in range(len(SENDERS)):
            ends.append(ends[-1] + count_ref[sender, group])

        here = pl.ds(pl.multiple_of(now * 2 * step, 2 * step), 2 * step)
        for row in range(rows_dev):
            sender, slot = 0, row
            for g in range(1, len(SENDERS)):
                later = row >= ends[g]
                sender = jnp.where(later, g, sender)
                slot = jnp.where(later, row - ends[g], slot)
            window = 0
            for j, flip in enumerate(SENDERS):
                window = jnp.where((sender ^ group) == flip, j, window)
            for half in range(2):
                at = jnp.where(row < ends[-1], 2 * SLOT * window + 2 * slot + half, blank)
                column = row * width + half * lanes
                for field in range(3):
                    block = held[at, field, here].astype(F32).reshape(step, 2, lanes)
                    out_ref[:, field, :, column : column + lanes] = block

    return pl.pallas_call(
        body,
        grid_spec=pltpu.PrefetchScalarGridSpec(
            num_scalar_prefetch=2,
            grid=(planes // step,),
            in_specs=[hbm_spec()] * len(held),
            out_specs=pl.BlockSpec((step, 3, 2, rows_dev * width), lambda i, *_: (i, 0, 0, 0)),
            scratch_shapes=[
                pltpu.VMEM((2 * SLOT * len(SENDERS) + 1, 3, depth, lanes), BF16),
                pltpu.SemaphoreType.DMA((planes // step, len(held))),
            ],
        ),
        out_shape=jax.ShapeDtypeStruct((planes, 3, 2, rows_dev * width), F32),
        compiler_params=PARAMS,
        cost_estimate=pl.CostEstimate(
            flops=0, bytes_accessed=rows_dev * 36 * planes * width, transcendentals=0
        ),
    )(me, count, *held)


def after(values, earlier):
    return list(lax.optimization_barrier((tuple(values), earlier))[0])


def permute(value, s, flip):
    devices, groups = lax.axis_size("gz"), lax.axis_size("ky")
    pairs = [(d * groups + g, (d ^ s) * groups + (g ^ flip)) for d in range(devices) for g in range(groups)]
    return lax.ppermute(value, ("gz", "ky"), pairs)


def exchange(buffers, flip):
    out = list(buffers)
    for s in reversed(range(0 if flip else 1, len(buffers))):
        out[s] = permute(buffers[s], s, flip)
    return out


def run(sizes, tables, fields, wall_operator, matrix, factors):
    devices = lax.axis_size("gz")
    me, _, count = tables
    pencils = []
    for flip, rows in zip(FLIPS, sizes):
        walled = wall_rows(flip, rows, devices, tables, fields, wall_operator)
        if sizes[0] < sizes[1]:
            tables = (after([me], walled[1])[0],) + tables[1:]
        pencils.append(exchange(walled, flip))
    first, second = (list(transform(me, pencil, matrix, factors)) for pencil in pencils)
    pieces = [(FLIPS[0], exchange(first, 0)), (FLIPS[1], exchange(second, 0))]
    if sizes[0] < sizes[1]:
        far, far_sent = windows(me, count, pieces[:1], [(2, 0), (2, 1)])
        near, near_sent = windows(me, count, pieces[1:], [(0, 0), (0, 1)])
    else:
        near_sent, far_sent = windows(me, count, pieces, [(0, 1), (2, 1)])
        near, far = windows(me, count, pieces, [(0, 0), (2, 0)])
    return near, far, permute(near_sent, 0, 1), permute(far_sent, 0, 1)


def per_device(fields, wall_operator, remap_offset, remap_count):
    devices = lax.axis_size("gz")
    half_z = fields.shape[0] * devices // 2
    matrix = jnp.asarray(mode_matrix(half_z))
    factors = jnp.asarray(mode_factors(half_z))
    width = wall_operator.shape[0]
    rows_dev = fields.shape[3] // width
    me = jnp.stack([lax.axis_index("gz"), lax.axis_index("ky")]).astype(jnp.int32)
    tables = (me, remap_offset, remap_count)
    sizes = [size for size in (12, 16) if 2 * size % devices == 0]
    branches = [functools.partial(run, (far, near)) for far in sizes for near in sizes]
    arguments = (tables, fields, wall_operator, matrix, factors)
    if len(branches) == 1:
        held = branches[0](*arguments)
    else:
        held = lax.switch(choose(remap_count, sizes), branches, *arguments)
    return place_rows(me, remap_count, held, rows_dev, width)


def solution(mesh):
    placed = (P("gz", None, None, "ky"), P(), P(), P())
    return jax.shard_map(
        per_device, mesh=mesh, in_specs=placed, out_specs=P("gz", None, None, "ky"), check_vma=False
    )
```

```python
import functools
import math

import jax
import jax.numpy as jnp
import ml_dtypes
import numpy as np
from jax import lax
from jax.experimental import pallas as pl
from jax.experimental.pallas import tpu as pltpu
from jax.sharding import PartitionSpec as P

NU_COEF = 0.05
STEP_DT = 0.3
SLOT = 8
LANES = 128
FLIPS = (2, 0)
SENDERS = (0, 2, 1, 3)
BF16 = jnp.bfloat16
F32 = jnp.float32
PARAMS = pltpu.CompilerParams(vmem_limit_bytes=56 * 2**20)


def mode_matrix(half_z):
    row = np.arange(half_z)[:, None]
    column = np.arange(half_z)[None, :]
    norm = math.sqrt(2.0 / half_z)
    step = math.pi / (2 * half_z)
    cosine = norm * np.cos(((row * (2 * column + 1)) % (4 * half_z)) * step)
    sine = norm * np.sin((((row + 1) * (2 * (half_z - 1 - column) + 1)) % (4 * half_z)) * step)
    cosine = cosine.astype(np.float32).astype(ml_dtypes.bfloat16).astype(np.float32)
    sine = sine.astype(np.float32).astype(ml_dtypes.bfloat16).astype(np.float32)
    top = np.concatenate([0.5 * cosine, 0.5 * cosine[:, ::-1]], axis=1)
    bottom = np.concatenate([0.5 * sine[:, ::-1], -0.5 * sine], axis=1)
    whole = np.concatenate([top, bottom], axis=0)
    return np.kron(whole, np.eye(2, dtype=np.float32)).astype(ml_dtypes.bfloat16)


def mode_factors(half_z):
    index = np.arange(2 * half_z)
    wave = np.where(index < half_z, index, index - half_z + 1) * (math.pi / half_z)
    pair = np.stack([np.exp(-NU_COEF * wave * wave), STEP_DT * wave]).astype(np.float32)
    return np.broadcast_to(np.repeat(pair, 2, axis=1)[:, :, None], (2, 4 * half_z, LANES)).copy()


def sent_runs(count, group, flip):
    first = count[group, group ^ flip]
    return first, first + count[group, group ^ flip ^ 1]


def choose(count, sizes):
    def body(count_ref, out_ref):
        choice = 0
        for flip in FLIPS:
            most = 0
            for group in range(4):
                most = jnp.maximum(most, sent_runs(count_ref, group, flip)[1])
            choice = choice * len(sizes) + sum((most > size).astype(jnp.int32) for size in sizes[:-1])
        out_ref[0] = choice

    smem = pl.BlockSpec(memory_space=pltpu.SMEM)
    return pl.pallas_call(
        body, in_specs=[smem], out_specs=smem, out_shape=jax.ShapeDtypeStruct((1,), jnp.int32)
    )(count)[0]


def hbm_spec():
    return pl.BlockSpec(memory_space=pl.ANY)


def whole_spec(shape):
    return pl.BlockSpec(shape, lambda *_: (0,) * len(shape))


def wall_rows(flip, rows, devices, tables, fields, wall_operator):
    width = wall_operator.shape[0]
    planes = fields.shape[0]
    depth = 2 * planes
    units = 2 * rows // devices
    strip = 3 * depth

    def body(me_ref, offset_ref, count_ref, fields_ref, wall_ref, *refs):
        outs, held = refs[:-1], refs[-1]
        me, group = me_ref[0], me_ref[1]
        middle, end = sent_runs(count_ref, group, flip)
        begins = offset_ref[group, group ^ flip], offset_ref[group, group ^ flip ^ 1] - middle

        def source(i):
            return jnp.where(i < end, i + jnp.where(i < middle, begins[0], begins[1]), 0)

        for s in range(0, devices, 2):
            for u in range(units):
                row = source(u * (devices // 2) + lax.shift_right_logical(me ^ s, 1))
                column = pl.multiple_of(row * width, width)
                for field in range(3):
                    at = u * strip + field * depth
                    held[at : at + depth] = fields_ref[:, field, :, pl.ds(column, width)].reshape(depth, width)
            walled = jnp.dot(held[...], wall_ref[...], preferred_element_type=F32).astype(BF16)
            halves = walled[:, :LANES], walled[:, LANES:]
            swapped = (me & 1) == 1
            for t in range(2):
                block = jnp.where(swapped, halves[1 - t], halves[t])
                for u in range(units):
                    for field in range(3):
                        at = u * strip + field * depth
                        outs[s + t][u, field] = block[at : at + depth]

    shape = (units, 3, depth, LANES)
    return pl.pallas_call(
        body,
        grid_spec=pltpu.PrefetchScalarGridSpec(
            num_scalar_prefetch=3,
            grid=(1,),
            in_specs=[whole_spec(fields.shape), whole_spec(wall_operator.shape)],
            out_specs=[whole_spec(shape)] * devices,
            scratch_shapes=[pltpu.VMEM((units * strip, width), BF16)],
        ),
        out_shape=[jax.ShapeDtypeStruct(shape, BF16)] * devices,
        compiler_params=PARAMS,
        cost_estimate=pl.CostEstimate(
            flops=rows * 12 * planes * width * width, bytes_accessed=12 * planes * width * (rows + 32), transcendentals=0
        ),
    )(*tables, fields, wall_operator)


def transform(me, pencil, matrix, factors):
    devices = len(pencil)
    units, _, depth, lanes = pencil[0].shape
    size = devices * depth
    strip = 3 * lanes

    def body(me_ref, *refs):
        ins, (matrix_ref, factors_ref) = refs[:devices], refs[devices : devices + 2]
        outs, (block, turned, scale) = refs[devices + 2 : -3], refs[-3:]
        for s in range(devices):
            at = pl.ds(pl.multiple_of((me_ref[0] ^ s) * depth, depth), depth)
            turned[s * depth : (s + 1) * depth] = matrix_ref[at]
            for k in range(2):
                scale[k, s * depth : (s + 1) * depth] = factors_ref[k, at]
            for u in range(units):
                for f in range(3):
                    column = u * strip + f * lanes
                    block[at, column : column + lanes] = ins[s][u, f]
        for u in range(units):
            modes = jnp.dot(turned[...], block[:, u * strip : (u + 1) * strip], preferred_element_type=F32)
            velocity, buoyant, magnetic = (modes[:, f * lanes : f * lanes + lanes] for f in range(3))
            damping, wave = scale[0], scale[1]
            coupled = (
                damping * (velocity + STEP_DT * buoyant + wave * magnetic),
                damping * (buoyant - STEP_DT * velocity),
                damping * (magnetic - wave * velocity),
            )
            for f in range(3):
                rounded = coupled[f].astype(BF16)
                for s in range(devices):
                    outs[s][u, f] = rounded[s * depth : (s + 1) * depth]

    spec = whole_spec(pencil[0].shape)
    return pl.pallas_call(
        body,
        grid_spec=pltpu.PrefetchScalarGridSpec(
            num_scalar_prefetch=1,
            grid=(1,),
            in_specs=[spec] * devices + [whole_spec(matrix.shape), whole_spec(factors.shape)],
            out_specs=[spec] * devices,
            scratch_shapes=[
                pltpu.VMEM((size, units * strip), BF16),
                pltpu.VMEM((size, size), BF16),
                pltpu.VMEM((2, size, lanes), F32),
            ],
        ),
        out_shape=[jax.ShapeDtypeStruct(pencil[0].shape, BF16)] * devices,
        compiler_params=PARAMS,
        cost_estimate=pl.CostEstimate(
            flops=units * 6 * size * size * lanes, bytes_accessed=units * 12 * size * lanes, transcendentals=0
        ),
    )(me, *pencil, matrix, factors)


def bring(buffers, held, sem):
    copies, first = [], 0
    for b, buffer in enumerate(buffers):
        size = buffer.shape[0]
        copies.append(pltpu.make_async_copy(buffer, held.at[pl.ds(first, size)], sem.at[b]))
        first += size
    for copy in copies:
        copy.start()
    return copies


def windows(me, count, pieces, wanted):
    buffers = [b for _, piece in pieces for b in piece]
    sizes = [sum(b.shape[0] for b in piece) for _, piece in pieces]
    bases = {flip: sum(sizes[:p]) for p, (flip, _) in enumerate(pieces)}
    units = {flip: piece[0].shape[0] for flip, piece in pieces}
    devices = len(pieces[0][1])
    unit_shape = buffers[0].shape[1:]
    shape = (2 * SLOT,) + unit_shape

    def body(me_ref, count_ref, *refs):
        ins, outs, (held, sem) = refs[: len(buffers)], refs[len(buffers) : -2], refs[-2:]
        copies = bring(ins, held, sem)
        group = me_ref[1]
        starts = {(flip, 0): 0 for flip, _ in pieces}
        starts |= {(flip, 1): 2 * sent_runs(count_ref, group ^ flip, flip)[0] for flip, _ in pieces}
        for copy in copies:
            copy.wait()
        for out, (flip, to) in zip(outs, wanted):
            for slot in range(2 * SLOT):
                unit = jnp.minimum(starts[flip, to] + slot, devices * units[flip] - 1)
                owner = (unit & (devices - 1)) ^ me_ref[0]
                level = lax.shift_right_logical(unit, devices.bit_length() - 1)
                out[slot] = held[bases[flip] + owner * units[flip] + level]

    return pl.pallas_call(
        body,
        grid_spec=pltpu.PrefetchScalarGridSpec(
            num_scalar_prefetch=2,
            grid=(1,),
            in_specs=[hbm_spec()] * len(buffers),
            out_specs=[whole_spec(shape)] * len(wanted),
            scratch_shapes=[pltpu.VMEM((sum(sizes),) + unit_shape, BF16), pltpu.SemaphoreType.DMA((len(buffers),))],
        ),
        out_shape=[jax.ShapeDtypeStruct(shape, BF16)] * len(wanted),
        compiler_params=PARAMS,
        cost_estimate=pl.CostEstimate(flops=0, bytes_accessed=2**21 * len(wanted), transcendentals=0),
    )(me, count, *buffers)


def place_rows(me, count, held, rows_dev, width):
    _, _, depth, lanes = held[0].shape
    planes, step = depth // 2, 8

    def body(me_ref, count_ref, *refs):
        ins, out_ref, (held, units, sem) = refs[:-4], refs[-4], refs[-3:]
        group = me_ref[1]
        blank = 2 * SLOT * len(SENDERS)

        now = pl.program_id(0)

        def copies(i):
            planes_of = pl.ds(pl.multiple_of(i * 2 * step, 2 * step), 2 * step)
            return [
                pltpu.make_async_copy(
                    ref.at[:, :, planes_of], held.at[pl.ds(2 * SLOT * w, 2 * SLOT), :, planes_of], sem.at[i, w]
                )
                for w, ref in enumerate(ins)
            ]

        @pl.when(now == 0)
        def _():
            for i in range(planes // step):
                for copy in copies(i):
                    copy.start()
            held[blank : blank + 2] = jnp.zeros((2,) + held.shape[1:], BF16)

            ends = [0]
            for sender in range(len(SENDERS)):
                ends.append(ends[-1] + count_ref[sender, group])
            for row in range(rows_dev):
                sender, slot = 0, row
                for g in range(1, len(SENDERS)):
                    later = row >= ends[g]
                    sender = jnp.where(later, g, sender)
                    slot = jnp.where(later, row - ends[g], slot)
                window = 0
                for j, flip in enumerate(SENDERS):
                    window = jnp.where((sender ^ group) == flip, j, window)
                units[row] = jnp.where(row < ends[-1], 2 * (SLOT * window + slot), blank)

        for copy in copies(now):
            copy.wait()
        here = pl.ds(pl.multiple_of(now * 2 * step, 2 * step), 2 * step)
        for row in range(rows_dev):
            for half in range(2):
                at = units[row] + half
                column = row * width + half * lanes
                for field in range(3):
                    block = held[at, field, here].astype(F32).reshape(step, 2, lanes)
                    out_ref[:, field, :, column : column + lanes] = block

    return pl.pallas_call(
        body,
        grid_spec=pltpu.PrefetchScalarGridSpec(
            num_scalar_prefetch=2,
            grid=(planes // step,),
            in_specs=[hbm_spec()] * len(held),
            out_specs=pl.BlockSpec((step, 3, 2, rows_dev * width), lambda i, *_: (i, 0, 0, 0)),
            scratch_shapes=[
                pltpu.VMEM((2 * SLOT * len(SENDERS) + 2, 3, depth, lanes), BF16),
                pltpu.SMEM((rows_dev,), jnp.int32),
                pltpu.SemaphoreType.DMA((planes // step, len(held))),
            ],
        ),
        out_shape=jax.ShapeDtypeStruct((planes, 3, 2, rows_dev * width), F32),
        compiler_params=PARAMS,
        cost_estimate=pl.CostEstimate(
            flops=0, bytes_accessed=rows_dev * 36 * planes * width, transcendentals=0
        ),
    )(me, count, *held)


def after(values, earlier):
    return list(lax.optimization_barrier((tuple(values), earlier))[0])


def permute(value, s, flip):
    devices, groups = lax.axis_size("gz"), lax.axis_size("ky")
    pairs = [(d * groups + g, (d ^ s) * groups + (g ^ flip)) for d in range(devices) for g in range(groups)]
    return lax.ppermute(value, ("gz", "ky"), pairs)


def exchange(buffers, flip):
    out = list(buffers)
    for s in reversed(range(0 if flip else 1, len(buffers))):
        out[s] = permute(buffers[s], s, flip)
    return out


def run(sizes, tables, fields, wall_operator, matrix, factors):
    devices = lax.axis_size("gz")
    me, _, count = tables
    pencils = []
    for flip, rows in zip(FLIPS, sizes):
        walled = wall_rows(flip, rows, devices, tables, fields, wall_operator)
        if sizes[0] < sizes[1]:
            tables = (after([me], walled[1])[0],) + tables[1:]
        pencils.append(exchange(walled, flip))
    first, second = (list(transform(me, pencil, matrix, factors)) for pencil in pencils)
    pieces = [(FLIPS[0], exchange(first, 0)), (FLIPS[1], exchange(second, 0))]
    if sizes[0] < sizes[1]:
        far, far_sent = windows(me, count, pieces[:1], [(2, 0), (2, 1)])
        near, near_sent = windows(me, count, pieces[1:], [(0, 0), (0, 1)])
    else:
        near_sent, far_sent = windows(me, count, pieces, [(0, 1), (2, 1)])
        near, far = windows(me, count, pieces, [(0, 0), (2, 0)])
    return near, far, permute(near_sent, 0, 1), permute(far_sent, 0, 1)


def per_device(fields, wall_operator, remap_offset, remap_count):
    devices = lax.axis_size("gz")
    half_z = fields.shape[0] * devices // 2
    matrix = jnp.asarray(mode_matrix(half_z))
    factors = jnp.asarray(mode_factors(half_z))
    width = wall_operator.shape[0]
    rows_dev = fields.shape[3] // width
    me = jnp.stack([lax.axis_index("gz"), lax.axis_index("ky")]).astype(jnp.int32)
    tables = (me, remap_offset, remap_count)
    sizes = [size for size in (12, 16) if 2 * size % devices == 0]
    branches = [functools.partial(run, (far, near)) for far in sizes for near in sizes]
    arguments = (tables, fields, wall_operator, matrix, factors)
    if len(branches) == 1:
        held = branches[0](*arguments)
    else:
        held = lax.switch(choose(remap_count, sizes), branches, *arguments)
    return place_rows(me, remap_count, held, rows_dev, width)


def solution(mesh):
    placed = (P("gz", None, None, "ky"), P(), P(), P())
    return jax.shard_map(
        per_device, mesh=mesh, in_specs=placed, out_specs=P("gz", None, None, "ky"), check_vma=False
    )
```

```python
import functools
import math

import jax
import jax.numpy as jnp
import ml_dtypes
import numpy as np
from jax import lax
from jax.experimental import pallas as pl
from jax.experimental.pallas import tpu as pltpu
from jax.sharding import PartitionSpec as P

NU_COEF = 0.05
STEP_DT = 0.3
SLOT = 8
LANES = 128
FLIPS = (2, 0)
SENDERS = (0, 2, 1, 3)
BF16 = jnp.bfloat16
F32 = jnp.float32
PARAMS = pltpu.CompilerParams(vmem_limit_bytes=56 * 2**20)


def mode_matrix(half_z):
    row = np.arange(half_z)[:, None]
    column = np.arange(half_z)[None, :]
    norm = math.sqrt(2.0 / half_z)
    step = math.pi / (2 * half_z)
    cosine = norm * np.cos(((row * (2 * column + 1)) % (4 * half_z)) * step)
    sine = norm * np.sin((((row + 1) * (2 * (half_z - 1 - column) + 1)) % (4 * half_z)) * step)
    cosine = cosine.astype(np.float32).astype(ml_dtypes.bfloat16).astype(np.float32)
    sine = sine.astype(np.float32).astype(ml_dtypes.bfloat16).astype(np.float32)
    top = np.concatenate([0.5 * cosine, 0.5 * cosine[:, ::-1]], axis=1)
    bottom = np.concatenate([0.5 * sine[:, ::-1], -0.5 * sine], axis=1)
    whole = np.concatenate([top, bottom], axis=0)
    return np.kron(whole, np.eye(2, dtype=np.float32)).astype(ml_dtypes.bfloat16)


def mode_factors(half_z):
    index = np.arange(2 * half_z)
    wave = np.where(index < half_z, index, index - half_z + 1) * (math.pi / half_z)
    pair = np.stack([np.exp(-NU_COEF * wave * wave), STEP_DT * wave]).astype(np.float32)
    return np.broadcast_to(np.repeat(pair, 2, axis=1)[:, :, None], (2, 4 * half_z, LANES)).copy()


def sent_runs(count, group, flip):
    first = count[group, group ^ flip]
    return first, first + count[group, group ^ flip ^ 1]


def choose(count, sizes):
    def body(count_ref, out_ref):
        choice = 0
        for flip in FLIPS:
            most = 0
            for group in range(4):
                most = jnp.maximum(most, sent_runs(count_ref, group, flip)[1])
            choice = choice * len(sizes) + sum((most > size).astype(jnp.int32) for size in sizes[:-1])
        out_ref[0] = lax.axis_index("gz")
        out_ref[1] = lax.axis_index("ky")
        out_ref[2] = choice

    smem = pl.BlockSpec(memory_space=pltpu.SMEM)
    return pl.pallas_call(
        body, in_specs=[smem], out_specs=smem, out_shape=jax.ShapeDtypeStruct((3,), jnp.int32)
    )(count)


def hbm_spec():
    return pl.BlockSpec(memory_space=pl.ANY)


def whole_spec(shape):
    return pl.BlockSpec(shape, lambda *_: (0,) * len(shape))


def wall_rows(flip, rows, devices, tables, fields, wall_operator):
    width = wall_operator.shape[0]
    planes = fields.shape[0]
    depth = 2 * planes
    units = 2 * rows // devices
    strip = 3 * depth

    def body(me_ref, offset_ref, count_ref, fields_ref, wall_ref, *refs):
        outs, held = refs[:-1], refs[-1]
        me, group = me_ref[0], me_ref[1]
        middle, end = sent_runs(count_ref, group, flip)
        begins = offset_ref[group, group ^ flip], offset_ref[group, group ^ flip ^ 1] - middle

        def source(i):
            return jnp.where(i < end, i + jnp.where(i < middle, begins[0], begins[1]), 0)

        for s in range(0, devices, 2):
            for u in range(units):
                row = source(u * (devices // 2) + lax.shift_right_logical(me ^ s, 1))
                column = pl.multiple_of(row * width, width)
                for field in range(3):
                    at = u * strip + field * depth
                    held[at : at + depth] = fields_ref[:, field, :, pl.ds(column, width)].reshape(depth, width)
            walled = jnp.dot(held[...], wall_ref[...], preferred_element_type=F32).astype(BF16)
            halves = walled[:, :LANES], walled[:, LANES:]
            swapped = (me & 1) == 1
            for t in range(2):
                block = jnp.where(swapped, halves[1 - t], halves[t])
                for u in range(units):
                    for field in range(3):
                        at = u * strip + field * depth
                        outs[s + t][u, field] = block[at : at + depth]

    shape = (units, 3, depth, LANES)
    return pl.pallas_call(
        body,
        grid_spec=pltpu.PrefetchScalarGridSpec(
            num_scalar_prefetch=3,
            grid=(1,),
            in_specs=[whole_spec(fields.shape), whole_spec(wall_operator.shape)],
            out_specs=[whole_spec(shape)] * devices,
            scratch_shapes=[pltpu.VMEM((units * strip, width), BF16)],
        ),
        out_shape=[jax.ShapeDtypeStruct(shape, BF16)] * devices,
        compiler_params=PARAMS,
        cost_estimate=pl.CostEstimate(
            flops=rows * 12 * planes * width * width, bytes_accessed=12 * planes * width * (rows + 32), transcendentals=0
        ),
    )(*tables, fields, wall_operator)


def transform(me, pencil, matrix, factors):
    devices = len(pencil)
    units, _, depth, lanes = pencil[0].shape
    size = devices * depth
    strip = 3 * lanes

    def body(me_ref, *refs):
        ins, (matrix_ref, factors_ref) = refs[:devices], refs[devices : devices + 2]
        outs, (block, turned, scale) = refs[devices + 2 : -3], refs[-3:]
        for s in range(devices):
            at = pl.ds(pl.multiple_of((me_ref[0] ^ s) * depth, depth), depth)
            turned[s * depth : (s + 1) * depth] = matrix_ref[at]
            for k in range(2):
                scale[k, s * depth : (s + 1) * depth] = factors_ref[k, at]
            for u in range(units):
                for f in range(3):
                    column = u * strip + f * lanes
                    block[at, column : column + lanes] = ins[s][u, f]
        for u in range(units):
            modes = jnp.dot(turned[...], block[:, u * strip : (u + 1) * strip], preferred_element_type=F32)
            velocity, buoyant, magnetic = (modes[:, f * lanes : f * lanes + lanes] for f in range(3))
            damping, wave = scale[0], scale[1]
            coupled = (
                damping * (velocity + STEP_DT * buoyant + wave * magnetic),
                damping * (buoyant - STEP_DT * velocity),
                damping * (magnetic - wave * velocity),
            )
            for f in range(3):
                rounded = coupled[f].astype(BF16)
                for s in range(devices):
                    outs[s][u, f] = rounded[s * depth : (s + 1) * depth]

    spec = whole_spec(pencil[0].shape)
    return pl.pallas_call(
        body,
        grid_spec=pltpu.PrefetchScalarGridSpec(
            num_scalar_prefetch=1,
            grid=(1,),
            in_specs=[spec] * devices + [whole_spec(matrix.shape), whole_spec(factors.shape)],
            out_specs=[spec] * devices,
            scratch_shapes=[
                pltpu.VMEM((size, units * strip), BF16),
                pltpu.VMEM((size, size), BF16),
                pltpu.VMEM((2, size, lanes), F32),
            ],
        ),
        out_shape=[jax.ShapeDtypeStruct(pencil[0].shape, BF16)] * devices,
        compiler_params=PARAMS,
        cost_estimate=pl.CostEstimate(
            flops=units * 6 * size * size * lanes, bytes_accessed=units * 12 * size * lanes, transcendentals=0
        ),
    )(me, *pencil, matrix, factors)


def bring(buffers, held, sem):
    copies, first = [], 0
    for b, buffer in enumerate(buffers):
        size = buffer.shape[0]
        copies.append(pltpu.make_async_copy(buffer, held.at[pl.ds(first, size)], sem.at[b]))
        first += size
    for copy in copies:
        copy.start()
    return copies


def windows(me, count, pieces, wanted):
    buffers = [b for _, piece in pieces for b in piece]
    sizes = [sum(b.shape[0] for b in piece) for _, piece in pieces]
    bases = {flip: sum(sizes[:p]) for p, (flip, _) in enumerate(pieces)}
    units = {flip: piece[0].shape[0] for flip, piece in pieces}
    devices = len(pieces[0][1])
    unit_shape = buffers[0].shape[1:]
    shape = (2 * SLOT,) + unit_shape

    def body(me_ref, count_ref, *refs):
        ins, outs, (held, sem) = refs[: len(buffers)], refs[len(buffers) : -2], refs[-2:]
        copies = bring(ins, held, sem)
        group = me_ref[1]
        starts = {(flip, 0): 0 for flip, _ in pieces}
        starts |= {(flip, 1): 2 * sent_runs(count_ref, group ^ flip, flip)[0] for flip, _ in pieces}
        for copy in copies:
            copy.wait()
        for out, (flip, to) in zip(outs, wanted):
            for slot in range(2 * SLOT):
                unit = jnp.minimum(starts[flip, to] + slot, devices * units[flip] - 1)
                owner = (unit & (devices - 1)) ^ me_ref[0]
                level = lax.shift_right_logical(unit, devices.bit_length() - 1)
                out[slot] = held[bases[flip] + owner * units[flip] + level]

    return pl.pallas_call(
        body,
        grid_spec=pltpu.PrefetchScalarGridSpec(
            num_scalar_prefetch=2,
            grid=(1,),
            in_specs=[hbm_spec()] * len(buffers),
            out_specs=[whole_spec(shape)] * len(wanted),
            scratch_shapes=[pltpu.VMEM((sum(sizes),) + unit_shape, BF16), pltpu.SemaphoreType.DMA((len(buffers),))],
        ),
        out_shape=[jax.ShapeDtypeStruct(shape, BF16)] * len(wanted),
        compiler_params=PARAMS,
        cost_estimate=pl.CostEstimate(flops=0, bytes_accessed=2**21 * len(wanted), transcendentals=0),
    )(me, count, *buffers)


def place_rows(me, count, held, rows_dev, width):
    _, _, depth, lanes = held[0].shape
    planes, step = depth // 2, 8

    def body(me_ref, count_ref, *refs):
        ins, out_ref, (held, units, sem) = refs[:-4], refs[-4], refs[-3:]
        group = me_ref[1]
        blank = 2 * SLOT * len(SENDERS)

        now = pl.program_id(0)

        def copies(i):
            planes_of = pl.ds(pl.multiple_of(i * 2 * step, 2 * step), 2 * step)
            return [
                pltpu.make_async_copy(
                    ref.at[:, :, planes_of], held.at[pl.ds(2 * SLOT * w, 2 * SLOT), :, planes_of], sem.at[i, w]
                )
                for w, ref in enumerate(ins)
            ]

        @pl.when(now == 0)
        def _():
            for i in range(planes // step):
                for copy in copies(i):
                    copy.start()
            held[blank : blank + 2] = jnp.zeros((2,) + held.shape[1:], BF16)

            ends = [0]
            for sender in range(len(SENDERS)):
                ends.append(ends[-1] + count_ref[sender, group])
            for row in range(rows_dev):
                sender, slot = 0, row
                for g in range(1, len(SENDERS)):
                    later = row >= ends[g]
                    sender = jnp.where(later, g, sender)
                    slot = jnp.where(later, row - ends[g], slot)
                window = 0
                for j, flip in enumerate(SENDERS):
                    window = jnp.where((sender ^ group) == flip, j, window)
                units[row] = jnp.where(row < ends[-1], 2 * (SLOT * window + slot), blank)

        for copy in copies(now):
            copy.wait()
        here = pl.ds(pl.multiple_of(now * 2 * step, 2 * step), 2 * step)
        for row in range(rows_dev):
            for half in range(2):
                at = units[row] + half
                column = row * width + half * lanes
                for field in range(3):
                    block = held[at, field, here].astype(F32).reshape(step, 2, lanes)
                    out_ref[:, field, :, column : column + lanes] = block

    return pl.pallas_call(
        body,
        grid_spec=pltpu.PrefetchScalarGridSpec(
            num_scalar_prefetch=2,
            grid=(planes // step,),
            in_specs=[hbm_spec()] * len(held),
            out_specs=pl.BlockSpec((step, 3, 2, rows_dev * width), lambda i, *_: (i, 0, 0, 0)),
            scratch_shapes=[
                pltpu.VMEM((2 * SLOT * len(SENDERS) + 2, 3, depth, lanes), BF16),
                pltpu.SMEM((rows_dev,), jnp.int32),
                pltpu.SemaphoreType.DMA((planes // step, len(held))),
            ],
        ),
        out_shape=jax.ShapeDtypeStruct((planes, 3, 2, rows_dev * width), F32),
        compiler_params=PARAMS,
        cost_estimate=pl.CostEstimate(
            flops=0, bytes_accessed=rows_dev * 36 * planes * width, transcendentals=0
        ),
    )(me, count, *held)


def after(values, earlier):
    return list(lax.optimization_barrier((tuple(values), earlier))[0])


def permute(value, s, flip):
    devices, groups = lax.axis_size("gz"), lax.axis_size("ky")
    pairs = [(d * groups + g, (d ^ s) * groups + (g ^ flip)) for d in range(devices) for g in range(groups)]
    return lax.ppermute(value, ("gz", "ky"), pairs)


def exchange(buffers, flip):
    out = list(buffers)
    for s in reversed(range(0 if flip else 1, len(buffers))):
        out[s] = permute(buffers[s], s, flip)
    return out


def run(sizes, tables, fields, wall_operator, matrix, factors):
    devices = lax.axis_size("gz")
    me, _, count = tables
    pencils = []
    for flip, rows in zip(FLIPS, sizes):
        walled = wall_rows(flip, rows, devices, tables, fields, wall_operator)
        if sizes[0] < sizes[1]:
            tables = (after([me], walled[1])[0],) + tables[1:]
        pencils.append(exchange(walled, flip))
    first, second = (list(transform(me, pencil, matrix, factors)) for pencil in pencils)
    pieces = [(FLIPS[0], exchange(first, 0)), (FLIPS[1], exchange(second, 0))]
    if sizes[0] < sizes[1]:
        far, far_sent = windows(me, count, pieces[:1], [(2, 0), (2, 1)])
        near, near_sent = windows(me, count, pieces[1:], [(0, 0), (0, 1)])
    else:
        near_sent, far_sent = windows(me, count, pieces, [(0, 1), (2, 1)])
        near, far = windows(me, count, pieces, [(0, 0), (2, 0)])
    return near, far, permute(near_sent, 0, 1), permute(far_sent, 0, 1)


def per_device(fields, wall_operator, remap_offset, remap_count):
    devices = lax.axis_size("gz")
    half_z = fields.shape[0] * devices // 2
    matrix = jnp.asarray(mode_matrix(half_z))
    factors = jnp.asarray(mode_factors(half_z))
    width = wall_operator.shape[0]
    rows_dev = fields.shape[3] // width
    sizes = [size for size in (12, 16) if 2 * size % devices == 0]
    me = choose(remap_count, sizes)
    tables = (me, remap_offset, remap_count)
    branches = [functools.partial(run, (far, near)) for far in sizes for near in sizes]
    arguments = (tables, fields, wall_operator, matrix, factors)
    if len(branches) == 1:
        held = branches[0](*arguments)
    else:
        held = lax.switch(me[2], branches, *arguments)
    return place_rows(me, remap_count, held, rows_dev, width)


def solution(mesh):
    placed = (P("gz", None, None, "ky"), P(), P(), P())
    return jax.shard_map(
        per_device, mesh=mesh, in_specs=placed, out_specs=P("gz", None, None, "ky"), check_vma=False
    )
```
